32 devices in a mesh: dp: 16 (over z, y, x), blk: 2 (over core).
Axes of the slice: x: 2, y: 2, z: 4, core: 2. Of those that a mesh axis runs over, the one named last changes fastest.
Arguments:
- tubes: bfloat16 [16, 1024, 768], P('dp', 'blk'), may hold values from -6 to 6
- tube_mask: int32 [16, 1024], P('dp', 'blk'), may hold values 0 or 1
- tube_order: int32 [16, 1024], P('dp', 'blk'), may hold values from 0 to 1023, each once within a row
- cotangent: bfloat16 [16, 1024, 768], P('dp', 'blk'), may hold values from -6 to 6
- mask_token: float32 [768], replicated, may hold values from -6 to 6
- pos_table: bfloat16 [1024, 768], replicated, may hold values from -3 to 3
- ln1_gain: float32 [768], replicated, may hold values from 0.5 to 1.5
- ln1_bias: float32 [768], replicated, may hold values from -3 to 3
- w_qkv: bfloat16 [768, 2304], replicated, may hold values from -0.21875 to 0.21875
- bias_q: float32 [768], replicated, may hold values from -3 to 3
- bias_v: float32 [768], replicated, may hold values from -3 to 3
- w_out: bfloat16 [768, 768], replicated, may hold values from -3.5 to 3.5
- bias_out: float32 [768], replicated, may hold values from -3 to 3
- ln2_gain: float32 [768], replicated, may hold values from 0.5 to 1.5
- ln2_bias: float32 [768], replicated, may hold values from -3 to 3
- w_up: bfloat16 [768, 3072], replicated, may hold values from -0.21875 to 0.21875
- bias_up: float32 [3072], replicated, may hold values from -3 to 3
- w_down: bfloat16 [3072, 768], replicated, may hold values from -0.109375 to 0.109375
- bias_down: float32 [768], replicated, may hold values from -3 to 3
Outputs:
- output: bfloat16 [16, 1024, 768], P('dp', 'blk')
- grad_tubes: float32 [16, 1024, 768], P('dp', 'blk')
- grad_mask_token: float32 [768], P(('dp', 'blk'))
- grad_pos_table: float32 [1024, 768], P(None, ('dp', 'blk'))
- grad_ln1_gain: float32 [768], P(('dp', 'blk'))
- grad_ln1_bias: float32 [768], P(('dp', 'blk'))
- grad_w_qkv: float32 [768, 2304], P(('dp', 'blk'))
- grad_bias_q: float32 [768], P(('dp', 'blk'))
- grad_bias_v: float32 [768], P(('dp', 'blk'))
- grad_w_out: float32 [768, 768], P(('dp', 'blk'))
- grad_bias_out: float32 [768], P(('dp', 'blk'))
- grad_ln2_gain: float32 [768], P(('dp', 'blk'))
- grad_ln2_bias: float32 [768], P(('dp', 'blk'))
- grad_w_up: float32 [768, 3072], P(('dp', 'blk'))
- grad_bias_up: float32 [3072], P(('dp', 'blk'))
- grad_w_down: float32 [3072, 768], P(('dp', 'blk'))
- grad_bias_down: float32 [768], P(('dp', 'blk'))
The draws below stay inside these ranges and needn't reach their ends.
Inputs may be any that keep to these rules, and one draw needn't show every extreme that they name: `tube_mask`: 1 marks a masked tube. `tube_order`: each clip's row is a permutation of 0 to 1023.
All inputs are finite; a program needn't handle non-finite values. No bound on the sum of `tube_mask` on one device may be relied on, other than what follows from the above.
Results may differ from the reference program's by a relative error of at most 0.019.
Values may be sent and summed in bfloat16 or wider, within the bound.
No kernel may reach another device: no remote copies, remote signals or barrier semaphores. Data moves between devices by JAX's collectives and lax.ppermute only.
A program may use at most 192 MiB of HBM per device.

```python
import jax
import jax.numpy as jnp
from jax import lax

D = 768
HEADS = 12
HEAD_DIM = 64
FF = 3072
LENGTH = 1024
CLIPS_ALL = 16


def with_ends(array, stream_key, least, largest):
    place = [jax.random.randint(jax.random.fold_in(stream_key, axis), (), 0, length) for axis, length in enumerate(array.shape)]
    longest = array.shape.index(max(array.shape))
    next_to = place[:longest] + [(place[longest] + 1) % array.shape[longest]] + place[longest + 1:]
    return array.at[tuple(place)].set(least).at[tuple(next_to)].set(largest)


def levels(rng, shape, cuts, least, largest):
    level, own = 1.0, jax.random.fold_in(rng, 6)
    for axis_at, shards_of in cuts:
        heights = jnp.exp(jax.random.uniform(jax.random.fold_in(own, axis_at), (shards_of,), jnp.float32, least / len(cuts), largest / len(cuts)))
        level = level * jnp.repeat(heights, shape[axis_at] // shards_of).reshape([-1 if axis == axis_at else 1 for axis in range(len(shape))])
    return level


def gaussian(stream_key, extent, scale, most, split=(), dtype=jnp.bfloat16):
    drawn = jax.random.normal(stream_key, extent, jnp.float32) * scale
    if len(split) > 0:
        drawn = levels(stream_key, extent, split, -0.22, 0.18) * drawn
    return jnp.clip(drawn, min=-most, max=most).astype(dtype)


def setup_inputs(seed: int = 0) -> dict:
    splits = jax.random.split(jax.random.key(seed), 20)
    return {
        "tubes": gaussian(splits[0], (CLIPS_ALL, LENGTH, D), 1.0, 6.0, ((0, 16), (1, 2))),
        "tube_mask": with_ends((jax.random.randint(splits[1], (CLIPS_ALL, LENGTH), 0, 5) < 2).astype(jnp.int32), jax.random.fold_in(splits[1], 1), 0, 1),
        "tube_order": jax.vmap(lambda own: jax.random.permutation(own, LENGTH))(jax.random.split(splits[2], CLIPS_ALL)).reshape((CLIPS_ALL, LENGTH)).astype(jnp.int32),
        "cotangent": gaussian(splits[3], (CLIPS_ALL, LENGTH, D), 1.0, 6.0, ((0, 16), (1, 2))),
        "mask_token": gaussian(splits[4], (D,), 1.0, 6.0, (), jnp.float32),
        "pos_table": gaussian(splits[5], (LENGTH, D), 0.5, 3.0),
        "ln1_gain": jnp.clip(1.0 + 0.1 * jax.random.normal(splits[6], (D,), jnp.float32), 0.5, 1.5),
        "ln1_bias": gaussian(splits[7], (D,), 0.5, 3.0, (), jnp.float32),
        "w_qkv": gaussian(splits[8], (D, 3 * D), D ** -0.5, 0.21875),
        "bias_q": gaussian(splits[9], (D,), 0.5, 3.0, (), jnp.float32),
        "bias_v": gaussian(splits[10], (D,), 0.5, 3.0, (), jnp.float32),
        "w_out": gaussian(splits[11], (D, D), (D // 256) ** -0.5, 3.5),
        "bias_out": gaussian(splits[12], (D,), 0.5, 3.0, (), jnp.float32),
        "ln2_gain": jnp.clip(1.0 + 0.1 * jax.random.normal(splits[13], (D,), jnp.float32), 0.5, 1.5),
        "ln2_bias": gaussian(splits[14], (D,), 0.5, 3.0, (), jnp.float32),
        "w_up": gaussian(splits[15], (D, FF), D ** -0.5, 0.21875),
        "bias_up": gaussian(splits[16], (FF,), 0.5, 3.0, (), jnp.float32),
        "w_down": gaussian(splits[17], (FF, D), FF ** -0.5, 0.109375),
        "bias_down": gaussian(splits[18], (D,), 0.5, 3.0, (), jnp.float32),
    }


epsilon = 1e-06
score_scale = 0.125

@jax.custom_vjp
def low(v):
    return lax.optimization_barrier(v.astype(jnp.bfloat16)).astype(jnp.float32)

@jax.custom_vjp
def low_back(v):
    return v

def low_keep(v):
    return (low(v), None)

def low_pass(kept, grad):
    return (grad,)

def back_keep(v):
    return (v, None)

def back_low(kept, grad):
    return (low(grad),)
low.defvjp(low_keep, low_pass)
low_back.defvjp(back_keep, back_low)

def matmul(left, right):
    return jnp.dot(left, right, precision=lax.Precision.HIGHEST)

def layer_norm(rows_in, gain_vec, shift_vec):
    row_mean = lax.optimization_barrier(jnp.mean(rows_in, -1, keepdims=True))
    centered = rows_in - row_mean
    variance = lax.optimization_barrier(jnp.mean(centered * centered, -1, keepdims=True))
    return centered * lax.rsqrt(variance + epsilon) * gain_vec + shift_vec

def attend(triple):
    queries, key_rows, values = triple
    scores = low_back(score_scale * jnp.einsum('qhd,khd->hqk', queries, key_rows, precision=lax.Precision.HIGHEST))
    row_max = lax.optimization_barrier(jnp.max(scores, -1, keepdims=True))
    exponent = jnp.exp(scores - row_max)
    probabilities = exponent / lax.optimization_barrier(jnp.sum(exponent, -1, keepdims=True))
    mixed = jnp.einsum('hqk,khd->qhd', low(probabilities), values, precision=lax.Precision.HIGHEST)
    return mixed.reshape(mixed.shape[0], -1)

def reference(tubes, tube_mask, tube_order, cotangent, mask_token, pos_table, ln1_gain, ln1_bias, w_qkv, bias_q, bias_v, w_out, bias_out, ln2_gain, ln2_bias, w_up, bias_up, w_down, bias_down):
    clip_count, length, model_width = tubes.shape
    masked = (tube_mask == 1)[..., None]

    def forward(tubes_f, token_vec, table_f, gain_one, shift_one, qkv_f, query_bias, value_bias, out_f, out_bias, gain_two, shift_two, up_f, up_bias, down_f, down_bias):
        embedded = jnp.where(masked, token_vec, tubes_f) + table_f[tube_order]
        flat_rows = embedded.reshape(-1, model_width)
        normed_one = low(layer_norm(flat_rows, gain_one, shift_one))
        packed = matmul(normed_one, qkv_f)
        queries = low_back(low(packed[:, :model_width] + query_bias))
        key_rows = low_back(low(packed[:, model_width:2 * model_width]))
        values = low_back(low(packed[:, 2 * model_width:] + value_bias))
        shape_four = (clip_count, length, HEADS, HEAD_DIM)
        attended = lax.map(jax.checkpoint(attend), (queries.reshape(shape_four), key_rows.reshape(shape_four), values.reshape(shape_four)))
        attended = low_back(low(attended.reshape(-1, model_width)))
        after_attn = flat_rows + low_back(matmul(attended, out_f) + out_bias)
        normed_two = low(layer_norm(after_attn, gain_two, shift_two))
        pre_act = low_back(matmul(normed_two, up_f) + up_bias)
        active = low(jax.nn.gelu(pre_act, approximate=False))
        result = after_attn + low_back(matmul(active, down_f) + down_bias)
        return result.reshape(clip_count, length, model_width)
    inputs = (tubes.astype(jnp.float32), mask_token.astype(jnp.float32), pos_table.astype(jnp.float32), ln1_gain.astype(jnp.float32), ln1_bias.astype(jnp.float32), w_qkv.astype(jnp.float32), bias_q.astype(jnp.float32), bias_v.astype(jnp.float32), w_out.astype(jnp.float32), bias_out.astype(jnp.float32), ln2_gain.astype(jnp.float32), ln2_bias.astype(jnp.float32), w_up.astype(jnp.float32), bias_up.astype(jnp.float32), w_down.astype(jnp.float32), bias_down.astype(jnp.float32))
    result, pull = jax.vjp(forward, *inputs)
    grads = pull(cotangent.astype(jnp.float32))
    return (result.astype(jnp.bfloat16), grads[0], grads[1], grads[2], grads[3], grads[4], grads[5], grads[6], grads[7], grads[8], grads[9], grads[10], grads[11], grads[12], grads[13], grads[14], grads[15])
```

```python
import functools
import math

import jax
import jax.numpy as jnp
from jax import lax
from jax.experimental import pallas as pl
from jax.experimental.pallas import tpu as pltpu
from jax.sharding import PartitionSpec as P

HEADS = 12
HEAD_DIM = 64
PAIR = 2 * HEAD_DIM
EPSILON = 1e-06
SCORE_SCALE = 0.125
OWNERS = 32
EXTRA = 128
BF = jnp.bfloat16
F32 = jnp.float32
ALL = ("dp", "blk")
MIB = 1 << 20

NN = (((1,), (0,)), ((), ()))
NT = (((1,), (1,)), ((), ()))
TN = (((0,), (0,)), ((), ()))


def dot(left, right, dims=NN):
    return lax.dot_general(left, right, dims, preferred_element_type=F32)


def params(mib, *semantics):
    return pltpu.CompilerParams(
        vmem_limit_bytes=mib * MIB,
        dimension_semantics=semantics or None,
    )


def normalize(rows):
    centered = rows - jnp.mean(rows, -1, keepdims=True)
    inverse = lax.rsqrt(jnp.mean(centered * centered, -1, keepdims=True) + EPSILON)
    return centered * inverse, inverse


def norm_backward(grad, unit, inverse, gain):
    scaled = grad * gain
    return inverse * (
        scaled
        - jnp.mean(scaled, -1, keepdims=True)
        - unit * jnp.mean(scaled * unit, -1, keepdims=True)
    )


def lane_columns(row):
    return jnp.transpose(jnp.broadcast_to(row, (128, row.shape[1])), (1, 0))


def place_blocks(perm_ref, transposed, slots):
    size = transposed.shape[0] // OWNERS
    for owner in range(OWNERS):
        slots[perm_ref[owner]] = transposed[owner * size : (owner + 1) * size]


def embed_kernel(
    steps_kv, order_ref, mask_ref, tubes_ref, token_ref, table_ref, gain_ref, shift_ref,
    w_ref, bias_ref, scale_ref, emb_ref, hot_ref, q_ref, kv_ref, normed,
):
    step = pl.program_id(0)

    @pl.when(step == 0)
    def _():
        order = lane_columns(order_ref[...])
        mask = lane_columns(mask_ref[...])
        width = tubes_ref.shape[1]
        lanes = lax.broadcasted_iota(jnp.int32, order.shape, 1).astype(F32)
        for at in range(0, table_ref.shape[0], 128):
            hot_ref[:, at : at + 128] = jnp.where(order == lanes + at, 1.0, 0.0).astype(BF)
        positions = dot(hot_ref[...], table_ref[...])
        masks = jnp.concatenate([mask] * (width // 128), 1)
        rows = jnp.where(masks > 0.5, token_ref[...], tubes_ref[...].astype(F32)) + positions
        emb_ref[...] = rows
        unit, _ = normalize(rows)
        normed[...] = (unit * gain_ref[...] + shift_ref[...]).astype(BF)

    packed = dot(normed[...], w_ref[...]) + bias_ref[...]

    @pl.when(step < steps_kv)
    def _():
        kv_ref[...] = packed.astype(BF)

    @pl.when(step >= steps_kv)
    def _():
        q_ref[...] = (packed.astype(BF).astype(F32) * scale_ref[...]).astype(BF)


def embed(order, mask, tubes, token, table, gain, shift, w_qkv, bias):
    rows, width = tubes.shape
    length = table.shape[0]
    tile = width // 2
    steps_q = width // tile
    steps_kv = 2 * steps_q
    steps = steps_q + steps_kv
    whole = lambda shape: pl.BlockSpec(shape, lambda j: (0,) * len(shape))
    column = lambda j: (0, lax.rem(j + steps_q, steps))
    scale = jnp.full((1, tile), SCORE_SCALE, F32)
    return pl.pallas_call(
        functools.partial(embed_kernel, steps_kv),
        grid=(steps,),
        in_specs=[
            whole((1, rows)), whole((1, rows)), whole((rows, width)), whole((1, width)),
            whole((length, width)), whole((1, width)), whole((1, width)),
            pl.BlockSpec((width, tile), column), pl.BlockSpec((1, tile), column),
            whole((1, tile)),
        ],
        out_specs=[
            whole((rows, width)), whole((rows, length)),
            pl.BlockSpec((rows, tile), lambda j: (0, jnp.maximum(j - steps_kv, 0))),
            pl.BlockSpec((rows, tile), lambda j: (0, jnp.minimum(j, steps_kv - 1))),
        ],
        out_shape=[
            jax.ShapeDtypeStruct((rows, width), F32),
            jax.ShapeDtypeStruct((rows, length), BF),
            jax.ShapeDtypeStruct((rows, width), BF),
            jax.ShapeDtypeStruct((rows, 2 * width), BF),
        ],
        scratch_shapes=[pltpu.VMEM((rows, width), BF)],
        compiler_params=params(40, "arbitrary"),
        name="embed",
    )(order, mask, tubes, token, table, gain, shift, w_qkv, bias, scale)


def attend_kernel(blocks, tile, *refs):
    q_ref, key_refs, value_refs = refs[0], refs[1 : 1 + blocks], refs[1 + blocks : 1 + 2 * blocks]
    out_ref, log_ref = refs[1 + 2 * blocks :]
    keys = jnp.concatenate([ref[...] for ref in key_refs], 0)
    values = jnp.concatenate([ref[...] for ref in value_refs], 0)
    low_half = lax.broadcasted_iota(jnp.int32, (1, PAIR), 1) < HEAD_DIM
    one, zero = jnp.ones((), BF), jnp.zeros((), BF)
    value_halves = [jnp.where(low_half, values, one), jnp.where(low_half, one, values)]
    for at in range(0, q_ref.shape[0], tile):
        queries = q_ref[at : at + tile, :]
        tops, mixed = [], []
        for half in range(2):
            own = jnp.where(low_half, queries, zero) if half == 0 else jnp.where(low_half, zero, queries)
            scores = dot(own, keys, NT)
            top = jnp.max(scores, -1, keepdims=True)
            weights = jnp.exp(scores - top).astype(BF)
            tops.append(top)
            mixed.append(dot(weights, value_halves[half]))
        total = pltpu.roll(jnp.where(low_half, mixed[1], mixed[0]), HEAD_DIM, 1)
        out_ref[at : at + tile, :] = jnp.where(low_half, mixed[0], mixed[1]) / total
        logs = jnp.where(low_half, tops[0], tops[1]) + jnp.log(total)
        logs = jnp.transpose(logs, (1, 0))
        log_ref[0, 0, 0:1, at : at + tile] = logs[0:1]
        log_ref[0, 0, 1:2, at : at + tile] = logs[HEAD_DIM : HEAD_DIM + 1]


def attend(queries, held, clips):
    rows, width = queries.shape
    block = rows // clips
    pairs = width // PAIR
    blocks = len(held)
    spec = lambda off: pl.BlockSpec((block, PAIR), lambda c, p: (c, p + off))
    return pl.pallas_call(
        functools.partial(attend_kernel, blocks, min(block, 256)),
        grid=(clips, pairs),
        in_specs=[spec(0)] + [spec(0)] * blocks + [spec(pairs)] * blocks,
        out_specs=[spec(0), pl.BlockSpec((1, 1, 2, block), lambda c, p: (c, p, 0, 0))],
        out_shape=[
            jax.ShapeDtypeStruct((rows, width), F32),
            jax.ShapeDtypeStruct((clips, pairs, 2, block), F32),
        ],
        compiler_params=params(40, "arbitrary", "arbitrary"),
        name="attend",
    )(queries, *held, *held)


def attend_back_kernel(blocks, tile, *refs):
    q_ref, grad_ref, out_ref, log_ref = refs[:4]
    key_refs, value_refs = refs[4 : 4 + blocks], refs[4 + blocks : 4 + 2 * blocks]
    refs = refs[4 + 2 * blocks :]
    dq_ref, dkey_refs, dvalue_refs = refs[0], refs[1 : 1 + blocks], refs[1 + blocks :]
    low_half = lax.broadcasted_iota(jnp.int32, (1, PAIR), 1) < HEAD_DIM
    zero = jnp.zeros((), BF)
    queries, grads = q_ref[...], grad_ref[...]
    product = jnp.transpose(grads.astype(F32) * out_ref[...], (1, 0))
    dots = [
        jnp.sum(product[half * HEAD_DIM : (half + 1) * HEAD_DIM], 0, keepdims=True)
        for half in range(2)
    ]
    logs = [log_ref[0, 0, half : half + 1, :] for half in range(2)]
    dq = jnp.zeros(queries.shape, F32)
    for block in range(blocks):
        for at in range(0, key_refs[block].shape[0], tile):
            keys = key_refs[block][at : at + tile, :]
            values = value_refs[block][at : at + tile, :]
            dkeys, dvalues = [], []
            for half in range(2):
                pick = lambda x: jnp.where(low_half, x, zero) if half == 0 else jnp.where(low_half, zero, x)
                own_keys = pick(keys)
                scores = dot(own_keys, queries, NT)
                probs = jnp.exp(scores - logs[half])
                grad_probs = dot(pick(values), grads, NT)
                grad_scores = (probs * (grad_probs - dots[half])).astype(BF)
                dvalues.append(dot(probs.astype(BF), grads))
                dkeys.append(dot(grad_scores, queries))
                dq += dot(grad_scores, own_keys, TN)
            dkey_refs[block][at : at + tile, :] = jnp.where(low_half, *dkeys).astype(dkey_refs[block].dtype)
            dvalue_refs[block][at : at + tile, :] = jnp.where(low_half, *dvalues).astype(dvalue_refs[block].dtype)
    dq_ref[...] = (dq * SCORE_SCALE).astype(BF)


def attend_back(queries, grads, attended, logs, held, clips):
    rows, width = queries.shape
    block = rows // clips
    pairs = width // PAIR
    blocks = len(held)
    spec = lambda off: pl.BlockSpec((block, PAIR), lambda c, p: (c, p + off))
    kinds = [F32] + [BF] * (blocks - 1)
    outs = pl.pallas_call(
        functools.partial(attend_back_kernel, blocks, min(block, 256)),
        grid=(clips, pairs),
        in_specs=[spec(0)] * 3
        + [pl.BlockSpec((1, 1, 2, block), lambda c, p: (c, p, 0, 0))]
        + [spec(0)] * blocks
        + [spec(pairs)] * blocks,
        out_specs=[spec(0)] * (1 + 2 * blocks),
        out_shape=[jax.ShapeDtypeStruct((rows, width), kind) for kind in [BF] + kinds + kinds],
        compiler_params=params(40, "arbitrary", "arbitrary"),
        name="attend_back",
    )(queries, grads, attended, logs, *held, *held)
    return outs[0], outs[1 : 1 + blocks], outs[1 + blocks :]


def gelu_terms(x):
    bell = jnp.exp(x * x * -0.5)
    t = 1.0 / (1.0 + jnp.abs(x) * (0.3275911 * math.sqrt(0.5)))
    a1, a2, a3, a4, a5 = (0.5 * a for a in (0.254829592, -0.284496736, 1.421413741, -1.453152027, 1.061405429))
    tail = t * (a1 + t * (a2 + t * (a3 + t * (a4 + t * a5)))) * bell
    cdf = jnp.where(x >= 0.0, 1.0 - tail, tail)
    return x * cdf, cdf + x * bell * (1.0 / math.sqrt(2.0 * math.pi))


def middle_kernel(
    steps, perm_ref, att_ref, emb_ref, cot_ref, w_out_ref, bias_out_ref, gain_ref, shift_ref,
    w_up_ref, bias_up_ref, w_down_ref, bias_down_ref,
    output_ref, grad_after_ref, branch_ref, grad_att_ref, att_t_ref, normed_t_ref, act_t_ref, grad_pre_ref,
    bias_up_grad_ref, small_ref,
    normed, unit, inverse, result, grad_normed, slots,
):
    step = pl.program_id(0)
    rows, width = att_ref.shape

    def to_slots(array, out_ref):
        place_blocks(perm_ref, jnp.transpose(array, (1, 0)), slots)
        out_ref[...] = slots[...].reshape(width, rows).astype(BF)

    @pl.when(step == 0)
    def _():
        attended = att_ref[...]
        after = emb_ref[...] + dot(attended.astype(BF), w_out_ref[...]) + bias_out_ref[...]
        unit_rows, inverse_rows = normalize(after)
        normed_rows = unit_rows * gain_ref[...] + shift_ref[...]
        normed[...] = normed_rows.astype(BF)
        unit[...] = unit_rows
        inverse[...] = jnp.broadcast_to(inverse_rows, inverse.shape)
        result[...] = after + bias_down_ref[...]
        grad_normed[...] = jnp.zeros_like(grad_normed)
        to_slots(attended, att_t_ref)
        to_slots(normed_rows, normed_t_ref)

    pre_act = dot(normed[...], w_up_ref[...]) + bias_up_ref[...]
    active, slope = gelu_terms(pre_act)
    result[...] += dot(active.astype(BF), w_down_ref[...])
    grad_pre = (dot(cot_ref[...], w_down_ref[...], NT) * slope).astype(BF)
    grad_pre_ref[...] = grad_pre
    grad_normed[...] += dot(grad_pre, w_up_ref[...], NT)
    bias_up_grad_ref[...] = jnp.sum(grad_pre.astype(F32), 0, keepdims=True)
    active_t = jnp.transpose(active, (1, 0)).astype(BF)
    count = OWNERS // steps
    size = active_t.shape[0] // count
    for i in range(count):
        act_t_ref[perm_ref[step * count + i]] = active_t[i * size : (i + 1) * size]

    @pl.when(step == steps - 1)
    def _():
        output_ref[...] = result[...].astype(BF)
        cot = cot_ref[...].astype(F32)
        grad_rows = grad_normed[...]
        unit_rows = unit[...]
        grad_after = cot + norm_backward(grad_rows, unit_rows, inverse[:, 0:1], gain_ref[...])
        grad_after_ref[...] = grad_after
        branch = grad_after.astype(BF)
        branch_ref[...] = branch
        grad_att_ref[...] = dot(branch, w_out_ref[...], NT).astype(BF)
        total = lambda x: jnp.sum(x, 0, keepdims=True)
        small_ref[...] = jnp.concatenate(
            [
                total(grad_rows * unit_rows), total(grad_rows), total(branch.astype(F32)), total(cot),
                jnp.zeros((4, width), F32),
            ],
            0,
        )


def middle(perm, attended, embedded, cot, w_out, bias_out, gain, shift, w_up, bias_up, w_down, bias_down):
    rows, width = attended.shape
    hidden = w_up.shape[1]
    steps = 8
    tile = hidden // steps
    whole = lambda shape: pl.BlockSpec(shape, lambda j, s: (0,) * len(shape))
    across = lambda n: pl.BlockSpec((n, tile), lambda j, s: (0, j))
    return pl.pallas_call(
        functools.partial(middle_kernel, steps),
        grid_spec=pltpu.PrefetchScalarGridSpec(
            num_scalar_prefetch=1,
            grid=(steps,),
            in_specs=[
                whole((rows, width)), whole((rows, width)), whole((rows, width)), whole((width, width)),
                whole((1, width)), whole((1, width)), whole((1, width)),
                across(width), across(1), pl.BlockSpec((tile, width), lambda j, s: (j, 0)), whole((1, width)),
            ],
            out_specs=[
                whole((rows, width)), whole((rows, width)), whole((rows, width)), whole((rows, width)),
                whole((width, rows)), whole((width, rows)), whole((OWNERS, hidden // OWNERS, rows)), across(rows),
                across(1), whole((8, width)),
            ],
            scratch_shapes=[
                pltpu.VMEM((rows, width), BF), pltpu.VMEM((rows, width), F32), pltpu.VMEM((rows, 128), F32),
                pltpu.VMEM((rows, width), F32), pltpu.VMEM((rows, width), F32),
                pltpu.VMEM((OWNERS, width // OWNERS, rows), F32),
            ],
        ),
        out_shape=[
            jax.ShapeDtypeStruct((rows, width), BF),
            jax.ShapeDtypeStruct((rows, width), F32),
            jax.ShapeDtypeStruct((rows, width), BF),
            jax.ShapeDtypeStruct((rows, width), BF),
            jax.ShapeDtypeStruct((width, rows), BF),
            jax.ShapeDtypeStruct((width, rows), BF),
            jax.ShapeDtypeStruct((OWNERS, hidden // OWNERS, rows), BF),
            jax.ShapeDtypeStruct((rows, hidden), BF),
            jax.ShapeDtypeStruct((1, hidden), F32),
            jax.ShapeDtypeStruct((8, width), F32),
        ],
        compiler_params=params(56, "arbitrary"),
        name="middle",
    )(perm, attended, embedded, cot, w_out, bias_out, gain, shift, w_up, bias_up, w_down, bias_down)


def pack_kernel(parts, perm_ref, emb_ref, gain_ref, shift_ref, dq_ref, *refs):
    dkey_refs, dvalue_refs = refs[:parts], refs[parts : 2 * parts]
    packed_ref, normed_t_ref, sums_ref, slots = refs[2 * parts :]
    rows, width = emb_ref.shape
    add = lambda group: functools.reduce(jnp.add, [ref[...].astype(F32) for ref in group]).astype(BF)
    dq, dvalue = dq_ref[...], add(dvalue_refs)
    packed_ref[:, :width] = dq
    packed_ref[:, width : 2 * width] = add(dkey_refs)
    packed_ref[:, 2 * width :] = dvalue
    total = lambda x: jnp.sum(x.astype(F32), 0, keepdims=True)
    sums_ref[...] = jnp.concatenate([total(dq), total(dvalue), jnp.zeros((6, width), F32)], 0)
    unit, _ = normalize(emb_ref[...])
    place_blocks(perm_ref, jnp.transpose(unit * gain_ref[...] + shift_ref[...], (1, 0)), slots)
    normed_t_ref[...] = slots[...].reshape(width, rows).astype(BF)


def pack(perm, embedded, gain, shift, dq, dkeys, dvalues):
    rows, width = embedded.shape
    vmem = pl.BlockSpec(memory_space=pltpu.VMEM)
    return pl.pallas_call(
        functools.partial(pack_kernel, len(dkeys)),
        in_specs=[pl.BlockSpec(memory_space=pltpu.SMEM)] + [vmem] * (4 + 2 * len(dkeys)),
        out_specs=[vmem] * 3,
        out_shape=[
            jax.ShapeDtypeStruct((rows, 3 * width), BF),
            jax.ShapeDtypeStruct((width, rows), BF),
            jax.ShapeDtypeStruct((8, width), F32),
        ],
        scratch_shapes=[pltpu.VMEM((OWNERS, width // OWNERS, rows), F32)],
        compiler_params=params(48),
        name="pack",
    )(perm, embedded, gain, shift, dq, *dkeys, *dvalues)


def last_kernel(
    steps, perm_ref, packed_ref, w_ref, emb_ref, grad_after_ref, mask_ref, gain_ref, sums_ref, small_ref, bias_up_ref,
    tubes_ref, grad_t_ref, extra_ref, grad_normed, slots, extra_slots,
):
    step = pl.program_id(0)
    rows, width = emb_ref.shape
    term = dot(packed_ref[...], w_ref[...], NT)

    @pl.when(step == 0)
    def _():
        grad_normed[...] = term

    @pl.when(step > 0)
    def _():
        grad_normed[...] += term

    @pl.when(step == steps - 1)
    def _():
        unit, inverse = normalize(emb_ref[...])
        grad_rows = grad_normed[...]
        grad = grad_after_ref[...] + norm_backward(grad_rows, unit, inverse, gain_ref[...])
        mask = lane_columns(mask_ref[...])
        masks = jnp.concatenate([mask] * (width // 128), 1) > 0.5
        tubes_ref[...] = jnp.where(masks, 0.0, grad)
        total = lambda x: jnp.sum(x, 0, keepdims=True)
        place_blocks(perm_ref, jnp.transpose(grad, (1, 0)), slots)
        grad_t_ref[...] = slots[...].reshape(width, rows).astype(BF)
        stacked = jnp.concatenate(
            [
                total(jnp.where(masks, grad, 0.0)), total(grad_rows * unit), total(grad_rows), sums_ref[0:2, :],
                small_ref[0:4, :], bias_up_ref[...], jnp.zeros((EXTRA - 13, width), F32),
            ],
            0,
        )
        place_blocks(perm_ref, jnp.transpose(stacked, (1, 0)), extra_slots)
        extra_ref[...] = extra_slots[...].reshape(width, EXTRA).astype(BF)


def last(perm, packed, w_qkv, embedded, grad_after, mask, gain, sums, small, bias_up_rows):
    rows, width = embedded.shape
    steps = 6
    tile = packed.shape[1] // steps
    whole = lambda shape: pl.BlockSpec(shape, lambda j, s: (0,) * len(shape))
    across = lambda n: pl.BlockSpec((n, tile), lambda j, s: (0, j))
    return pl.pallas_call(
        functools.partial(last_kernel, steps),
        grid_spec=pltpu.PrefetchScalarGridSpec(
            num_scalar_prefetch=1,
            grid=(steps,),
            in_specs=[
                across(rows), across(width), whole((rows, width)), whole((rows, width)), whole((1, rows)),
                whole((1, width)), whole((8, width)), whole((8, width)), whole((4, width)),
            ],
            out_specs=[whole((rows, width)), whole((width, rows)), whole((width, EXTRA))],
            scratch_shapes=[
                pltpu.VMEM((rows, width), F32),
                pltpu.VMEM((OWNERS, width // OWNERS, rows), F32),
                pltpu.VMEM((OWNERS, width // OWNERS, EXTRA), F32),
            ],
        ),
        out_shape=[
            jax.ShapeDtypeStruct((rows, width), F32),
            jax.ShapeDtypeStruct((width, rows), BF),
            jax.ShapeDtypeStruct((width, EXTRA), BF),
        ],
        compiler_params=params(48, "arbitrary"),
        name="last",
    )(perm, packed, w_qkv, embedded, grad_after, mask, gain, sums, small, bias_up_rows)


def swap(array, bit):
    if bit == 0:
        return lax.ppermute(array, "blk", [(0, 1), (1, 0)])
    step = 1 << (bit - 1)
    return lax.ppermute(array, "dp", [(i, i ^ step) for i in range(OWNERS // 2)])


ROW_BITS = (1, 2, 3, 4)


def halve(array, left, bit):
    at = left.index(bit)
    rows, columns = array.shape
    after = rows >> (at + 1)
    cut = array.reshape(1 << at, 2, after, columns)
    keep, send = cut[:, 0].reshape(rows // 2, columns), cut[:, 1].reshape(rows // 2, columns)
    received = swap(send, bit)
    total = keep.astype(F32) + received.astype(F32)
    return total, tuple(b for b in left if b != bit)


def reduce_chain(array, order):
    left = ROW_BITS
    for bit in order:
        array, left = halve(array.astype(BF), left, bit)
    return array


ORDERS = ((1, 2, 3, 4), (2, 1, 3, 4), (3, 1, 2, 4))


def weight_grad(left, right):
    rows = left.shape[0] // 2
    other = dot(left[rows:], right).astype(BF)
    received = swap(other, 0)
    return (dot(left[:rows], right) + received.astype(F32)).astype(BF)


def scatter_sum(array, parts):
    width = array.shape[1] // parts
    cuts = [array[:, i * width : (i + 1) * width] for i in range(parts)]
    return jnp.concatenate([reduce_chain(cut, ORDERS[i % 3]) for i, cut in enumerate(cuts)], 1)


def body(
    paired,
    tubes, tube_mask, tube_order, cotangent, mask_token, pos_table, ln1_gain, ln1_bias, w_qkv, bias_q, bias_v,
    w_out, bias_out, ln2_gain, ln2_bias, w_up, bias_up, w_down, bias_down,
):
    clips, block, width = tubes.shape
    rows = clips * block
    blocks = lax.axis_size("blk")
    devices = blocks * lax.axis_size("dp")
    row = lambda x: x.reshape(1, -1)
    owners = jnp.arange(OWNERS, dtype=jnp.int32)
    if paired:
        me = lax.axis_index("dp") * 2 + lax.axis_index("blk")
        apart = jnp.bitwise_xor(owners, me)
        perm = sum(((apart >> bit) & 1) << (4 - bit) for bit in range(5))
    else:
        perm = owners

    order = tube_order.reshape(1, rows).astype(F32)
    mask = tube_mask.reshape(1, rows).astype(F32)
    cot = cotangent.reshape(rows, width)
    bias = jnp.concatenate([bias_q, jnp.zeros_like(bias_q), bias_v]).reshape(1, -1)
    embedded, hot, queries, kv = embed(
        order, mask, tubes.reshape(rows, width), row(mask_token), pos_table, row(ln1_gain), row(ln1_bias), w_qkv, bias
    )
    held = [kv] + [
        lax.ppermute(kv, "blk", [(i, (i + s) % blocks) for i in range(blocks)]) for s in range(1, blocks)
    ]
    attended, logs = attend(queries, held, clips)
    (
        output, grad_after, branch, grad_att, att_t, normed_t, act_t, grad_pre, bias_up_grad, small,
    ) = middle(
        perm, attended, embedded, cot, w_out, row(bias_out), row(ln2_gain), row(ln2_bias), w_up, row(bias_up),
        w_down, row(bias_down),
    )
    act_t = act_t.reshape(-1, rows)
    if paired:
        total_down = weight_grad(act_t, cot)
        total_up = weight_grad(normed_t, grad_pre)
        total_out = weight_grad(att_t, branch)
        grad_w_down = scatter_sum(total_down, 3)
        grad_w_up = scatter_sum(total_up, 3)
        grad_w_out = scatter_sum(total_out, 1)
    else:
        spread = lambda left, right: lax.psum_scatter(dot(left, right), ALL, scatter_dimension=0, tiled=True)
        grad_w_down = spread(act_t, cot)
        grad_w_up = spread(normed_t, grad_pre)
        grad_w_out = spread(att_t, branch)

    dq, dkeys, dvalues = attend_back(queries, grad_att, attended, logs, held, clips)
    home = lambda x, s: lax.ppermute(x, "blk", [((i + s) % blocks, i) for i in range(blocks)])
    dkeys = [dkeys[0]] + [home(dkeys[s], s) for s in range(1, blocks)]
    dvalues = [dvalues[0]] + [home(dvalues[s], s) for s in range(1, blocks)]
    packed, normed_one_t, sums = pack(perm, embedded, row(ln1_gain), row(ln1_bias), dq, dkeys, dvalues)
    bias_up_rows = bias_up_grad.reshape(devices, -1, width // devices).swapaxes(0, 1).reshape(-1, width)
    grad_tubes, grad_t, extra = last(
        perm, packed, w_qkv, embedded, grad_after, mask, row(ln1_gain), sums, small, bias_up_rows
    )
    if paired:
        grad_w_qkv = scatter_sum(weight_grad(normed_one_t, packed), 3)
        total_pos = weight_grad(grad_t, hot)
        half = extra.shape[0] // 2
        total_extra = (extra[:half].astype(F32) + swap(extra[half:], 0).astype(F32)).astype(BF)
        tail = scatter_sum(jnp.concatenate([total_pos, total_extra], 1), 3)
        grad_pos, extra = tail[:, : hot.shape[1]], tail[:, hot.shape[1] :]
    else:
        grad_w_qkv = spread(normed_one_t, packed)
        grad_pos = spread(grad_t, hot)
        extra = lax.psum_scatter(extra.astype(F32), ALL, scatter_dimension=0, tiled=True)
    vector = [extra[:, i] for i in range(9)]
    grad_bias_up = extra[:, 9:13].T.reshape(-1)
    mask_grad, gain_one, shift_one, grad_bias_q, grad_bias_v, gain_two, shift_two, grad_bias_out, grad_bias_down = vector
    return (
        output.reshape(clips, block, width),
        grad_tubes.reshape(clips, block, width),
        mask_grad,
        grad_pos.T,
        gain_one,
        shift_one,
        grad_w_qkv,
        grad_bias_q,
        grad_bias_v,
        grad_w_out,
        grad_bias_out,
        gain_two,
        shift_two,
        grad_w_up,
        grad_bias_up,
        grad_w_down,
        grad_bias_down,
    )


def solution(mesh):
    split = P("dp", "blk", None)
    flat = P("dp", "blk")
    in_specs = (split, flat, flat, split) + (P(),) * 15
    one, two = P(ALL), P(ALL, None)
    out_specs = (split, split, one, P(None, ALL), one, one, two, one, one, two, one, one, one, two, one, two, one)
    paired = mesh.shape["blk"] == 2 and mesh.shape["dp"] == OWNERS // 2
    return jax.shard_map(
        functools.partial(body, paired), mesh=mesh, in_specs=in_specs, out_specs=out_specs, check_vma=False
    )
```

```python
import functools
import math

import jax
import jax.numpy as jnp
from jax import lax
from jax.experimental import pallas as pl
from jax.experimental.pallas import tpu as pltpu
from jax.sharding import PartitionSpec as P

HEADS = 12
HEAD_DIM = 64
PAIR = 2 * HEAD_DIM
EPSILON = 1e-06
SCORE_SCALE = 0.125
OWNERS = 32
EXTRA = 128
BF = jnp.bfloat16
F32 = jnp.float32
ALL = ("dp", "blk")
MIB = 1 << 20

NN = (((1,), (0,)), ((), ()))
NT = (((1,), (1,)), ((), ()))
TN = (((0,), (0,)), ((), ()))


def dot(left, right, dims=NN):
    return lax.dot_general(left, right, dims, preferred_element_type=F32)


def cost(micros):
    return pl.CostEstimate(flops=int(micros * 1e9), bytes_accessed=int(micros * 1e6), transcendentals=0)


def params(mib):
    return pltpu.CompilerParams(vmem_limit_bytes=mib * MIB)


def normalize(rows):
    centered = rows - jnp.mean(rows, -1, keepdims=True)
    inverse = lax.rsqrt(jnp.mean(centered * centered, -1, keepdims=True) + EPSILON)
    return centered * inverse, inverse


def norm_backward(grad, unit, inverse, gain):
    scaled = grad * gain
    return inverse * (
        scaled
        - jnp.mean(scaled, -1, keepdims=True)
        - unit * jnp.mean(scaled * unit, -1, keepdims=True)
    )


def lane_columns(row):
    return jnp.transpose(jnp.broadcast_to(row, (128, row.shape[1])), (1, 0))


def store_quarters(refs, array):
    quarter = array.shape[0] // 4
    for i, ref in enumerate(refs):
        ref[...] = array[i * quarter : (i + 1) * quarter].astype(BF)


SLOT, WITHIN, LAYER = 0, OWNERS, OWNERS + 8


def place_blocks(table_ref, transposed, slots):
    size = transposed.shape[0] // OWNERS
    for owner in range(OWNERS):
        slots[table_ref[SLOT + owner]] = transposed[owner * size : (owner + 1) * size]


def flat(ref):
    return ref[...].reshape(1, -1)


def add(terms):
    return functools.reduce(jnp.add, [x.astype(F32) for x in terms])


def total(rows):
    return jnp.sum(rows, 0, keepdims=True)


VMEM = pl.BlockSpec(memory_space=pltpu.VMEM)
SMEM = pl.BlockSpec(memory_space=pltpu.SMEM)
ANY = pl.BlockSpec(memory_space=pl.ANY)
HBM = pl.BlockSpec(memory_space=pltpu.HBM)


def in_hbm(array):
    return pltpu.with_memory_space_constraint(array, pltpu.HBM)


def one_hot(order_ref, length):
    order = lane_columns(order_ref[...].astype(F32))
    lanes = lax.broadcasted_iota(jnp.int32, order.shape, 1).astype(F32)
    return jnp.concatenate([jnp.where(order == lanes + at, 1.0, 0.0).astype(BF) for at in range(0, length, 128)], 1)


def wide_mask(mask_ref, width):
    mask = lane_columns(mask_ref[...].astype(F32))
    return jnp.concatenate([mask] * (width // 128), 1) > 0.5


def embed_kernel(table_ref, *refs):
    sources, refs = refs[:10], refs[10:]
    (emb_ref, normed_t_ref, q_ref, kv_ref), refs = refs[:4], refs[4:]
    places, (normed, slots, w, sems) = refs[:9], refs[9:]
    order_ref, mask_ref, positions_ref, tubes_ref, token_ref, gain_ref, shift_ref, bias_q_ref, bias_v_ref = places
    rows, width = tubes_ref.shape
    loads = [pltpu.make_async_copy(source, place, sems.at[i]) for i, (source, place) in enumerate(zip(sources, places))]
    w_ref = sources[9]
    loads += [
        pltpu.make_async_copy(w_ref.at[:, pl.ds(part * width, width)], w.at[part], sems.at[9 + part]) for part in range(3)
    ]
    for load in loads:
        load.start()
    loads[0].wait()
    hot = one_hot(order_ref, positions_ref.shape[0])
    for load in loads[1:9]:
        load.wait()
    masks = wide_mask(mask_ref, width)
    embedded = jnp.where(masks, flat(token_ref), tubes_ref[...].astype(F32)) + dot(hot, positions_ref[...])
    emb_ref[...] = embedded
    unit, _ = normalize(embedded)
    normed_rows = unit * flat(gain_ref) + flat(shift_ref)
    normed[...] = normed_rows.astype(BF)
    for load in loads[9:]:
        load.wait()
    kv_ref[:, :width] = dot(normed[...], w[1]).astype(BF)
    kv_ref[:, width:] = (dot(normed[...], w[2]) + flat(bias_v_ref)).astype(BF)
    queries = (dot(normed[...], w[0]) + flat(bias_q_ref)).astype(BF)
    q_ref[...] = (queries.astype(F32) * SCORE_SCALE).astype(BF)
    place_blocks(table_ref, jnp.transpose(normed_rows, (1, 0)), slots)
    normed_t_ref[...] = slots[...].reshape(width, rows).astype(BF)


def embed(table, order, mask, positions, tubes, vectors, w_qkv):
    rows, width = tubes.shape
    sources = (order, mask, positions, tubes, *vectors)
    return pl.pallas_call(
        embed_kernel,
        in_specs=[SMEM] + [HBM] * 10,
        out_specs=[VMEM] * 4,
        out_shape=[
            jax.ShapeDtypeStruct((rows, width), F32),
            jax.ShapeDtypeStruct((width, rows), BF),
            jax.ShapeDtypeStruct((rows, width), BF),
            jax.ShapeDtypeStruct((rows, 2 * width), BF),
        ],
        scratch_shapes=[pltpu.VMEM(x.shape, x.dtype) for x in sources]
        + [
            pltpu.VMEM((rows, width), BF),
            pltpu.VMEM((OWNERS, width // OWNERS, rows), F32),
            pltpu.VMEM((3, width, width), BF),
            pltpu.SemaphoreType.DMA((12,)),
        ],
        compiler_params=params(24),
        cost_estimate=cost(6),
        name="embed",
    )(table, *[in_hbm(x) for x in (*sources, w_qkv)])


def attend_pair(queries_ref, keys, values, tile, out_ref, log_ref):
    low_half = lax.broadcasted_iota(jnp.int32, (1, PAIR), 1) < HEAD_DIM
    one, zero = jnp.ones((), BF), jnp.zeros((), BF)
    value_halves = [jnp.where(low_half, values, one), jnp.where(low_half, one, values)]
    items = [(at, half) for at in range(0, queries_ref.shape[0], tile) for half in range(2)]

    def score(at, half):
        queries = queries_ref[at : at + tile, :]
        own = jnp.where(low_half, queries, zero) if half == 0 else jnp.where(low_half, zero, queries)
        return dot(own, keys, NT)

    ahead = score(*items[0])
    for i, (at, half) in enumerate(items):
        scores = ahead
        if i + 1 < len(items):
            ahead = score(*items[i + 1])
        if half == 0:
            tops, mixed = [], []
        top = jnp.max(scores, -1, keepdims=True)
        weights = jnp.exp(scores - top).astype(BF)
        tops.append(top)
        mixed.append(dot(weights, value_halves[half]))
        if half == 0:
            continue
        sums = pltpu.roll(jnp.where(low_half, mixed[1], mixed[0]), HEAD_DIM, 1)
        out_ref[at : at + tile, :] = jnp.where(low_half, mixed[0], mixed[1]) / sums
        logs = jnp.where(low_half, tops[0], tops[1]) + jnp.log(sums)
        logs = jnp.transpose(logs, (1, 0))
        log_ref[0:1, at : at + tile] = logs[0:1]
        log_ref[1:2, at : at + tile] = logs[HEAD_DIM : HEAD_DIM + 1]


def gelu_terms(x):
    bell = jnp.exp(x * x * -0.5)
    t = 1.0 / (1.0 + jnp.abs(x) * (0.3275911 * math.sqrt(0.5)))
    a1, a2, a3, a4, a5 = (0.5 * a for a in (0.254829592, -0.284496736, 1.421413741, -1.453152027, 1.061405429))
    tail = t * (a1 + t * (a2 + t * (a3 + t * (a4 + t * a5)))) * bell
    cdf = jnp.where(x >= 0.0, 1.0 - tail, tail)
    return x * cdf, cdf + x * bell * (1.0 / math.sqrt(2.0 * math.pi))


FF_STEPS = 4
NEAR_BLOCKS, FAR_BLOCKS = FF_STEPS + 1, FF_STEPS - 2


def pair_loop(clips, pairs, block, work):
    def step(i, carry):
        clip, pair = lax.div(i, pairs), lax.rem(i, pairs)
        at = pl.ds(pl.multiple_of(clip * block, block), block)
        work(clip, pair, at, lambda off: pl.ds(pl.multiple_of((pair + off) * PAIR, PAIR), PAIR))
        return carry

    lax.fori_loop(0, clips * pairs, step, 0)


def after_attention(att_ref, emb_ref, w_ref, bias_ref):
    return emb_ref[...] + dot(att_ref[...].astype(BF), w_ref[...]) + flat(bias_ref)


def forward_kernel(clips, blocks, tile, table_ref, q_ref, *refs):
    held_refs = refs[:blocks]
    (
        emb_ref, bias_out_ref, gain_ref, shift_ref, bias_in_ref, cot_ref, w_out_ref, w_up_ref, w_down_ref,
        att, log_ref, result, grad_normed, bias_up_ref,
    ) = refs[blocks : 14 + blocks]
    near_refs, middle_refs, far_refs = (refs[14 + blocks :][i:j] for i, j in ((0, 4), (4, 6), (6, 8)))
    normed, normed_t, slots, act_slots, w_up, w_down, stage, in_sems, out_sems = refs[22 + blocks :]
    rows, width = emb_ref.shape
    pairs = width // PAIR
    quarter = width // 4
    loads = []
    for f in range(FF_STEPS):
        at = pl.ds(f * width, width)
        loads.append(
            [
                pltpu.make_async_copy(w_up_ref.at[:, at], w_up.at[f], in_sems.at[f, 0]),
                pltpu.make_async_copy(w_down_ref.at[at, :], w_down.at[f], in_sems.at[f, 1]),
            ]
        )
        for load in loads[f]:
            load.start()

    def attend_one(clip, pair, at, lanes):
        keys = jnp.concatenate([ref[at, lanes(0)] for ref in held_refs], 0)
        values = jnp.concatenate([ref[at, lanes(pairs)] for ref in held_refs], 0)
        attend_pair(q_ref.at[at, lanes(0)], keys, values, tile, att.at[at, lanes(0)], log_ref.at[clip, pair])

    pair_loop(clips, pairs, rows // clips, attend_one)

    after = after_attention(att, emb_ref, w_out_ref, bias_out_ref)
    unit_rows, inverse_rows = normalize(after)
    normed_rows = unit_rows * flat(gain_ref) + flat(shift_ref)
    normed[...] = normed_rows.astype(BF)
    result[...] = after
    place_blocks(table_ref, jnp.transpose(normed_rows, (1, 0)), slots)
    normed_t[...] = slots[...].reshape(width, rows).astype(BF)

    stores = {}

    def store(f, kind, array):
        for old in stores.pop((kind, f % 2), ()):
            old.wait()
        copies = []
        parts = [array[i * quarter : (i + 1) * quarter] for i in range(4)]
        if kind == 0:
            targets = [ref.at[table_ref[LAYER + f]] for ref in near_refs]
        elif f == 0:
            targets = [ref.at[FF_STEPS] for ref in near_refs]
        elif f == 1:
            targets = [middle_refs[i // 2].at[pl.ds(i % 2 * quarter, quarter)] for i in range(4)]
        else:
            targets = [far_refs[i // 2].at[f - 2, pl.ds(i % 2 * quarter, quarter)] for i in range(4)]
            owner = width // OWNERS
            by_z = [i * 16 + xy * 4 + z for i in range(2) for z in range(4) for xy in range(4)]
            parts = [
                jnp.concatenate([array[slot * owner : (slot + 1) * owner] for slot in by_z[i * 8 : i * 8 + 8]], 0)
                for i in range(4)
            ]
        for i, (part, target) in enumerate(zip(parts, targets)):
            place = stage.at[kind, f % 2, i]
            place[...] = part.astype(BF)
            copies.append(pltpu.make_async_copy(place, target, out_sems.at[kind, f % 2, i]))
            copies[-1].start()
        stores[kind, f % 2] = copies

    size = width // 2

    def products(f, i):
        at = slice(i * size, (i + 1) * size)
        bias = flat(bias_in_ref)[:, f * width + i * size :][:, :size]
        return dot(normed[...], w_up[f, :, at]) + bias, dot(cot_ref[...], w_down[f, at, :], NT)

    def activate(f, i, pre_act, grad_active):
        active, slope = gelu_terms(pre_act)
        grad_pre = (grad_active * slope).astype(BF)
        bias_up_ref[f : f + 1, i * size : (i + 1) * size] = total(grad_pre.astype(F32))
        active_t = jnp.transpose(active, (1, 0)).astype(BF)
        for k in range(4):
            slot = table_ref[WITHIN + i * 4 + k]
            act_slots[f % 2, slot] = active_t[k * (size // 4) : (k + 1) * (size // 4)]
        return active.astype(BF), grad_pre

    def grad_up(f, grad_pre):
        store(f, 1, dot(normed_t[...], grad_pre))

    def grad_down(f):
        store(f, 0, dot(act_slots[f % 2].reshape(width, rows), cot_ref[...]))

    def add_up(f, active, grad_pre):
        result[...] += dot(active, w_down[f])
        term = dot(grad_pre, w_up[f], NT)
        if f == 0:
            grad_normed[...] = term
        else:
            grad_normed[...] += term

    held = None
    for f in range(FF_STEPS):
        for load in loads[f]:
            load.wait()
        ahead = [products(f, 0), products(f, 1)]
        if held:
            grad_up(f - 1, held[1])
        one = activate(f, 0, *ahead[0])
        if held:
            grad_down(f - 1)
        two = activate(f, 1, *ahead[1])
        if held:
            add_up(f - 1, *held)
        held = [jnp.concatenate(x, 1) for x in zip(one, two)]
    grad_up(FF_STEPS - 1, held[1])
    grad_down(FF_STEPS - 1)
    add_up(FF_STEPS - 1, *held)
    bias_up_ref[FF_STEPS:, :] = jnp.zeros((8 - FF_STEPS, width), F32)
    for copies in stores.values():
        for copy in copies:
            copy.wait()


def forward(table, queries, held, embedded, vectors, cot, w_out, w_up, w_down, clips):
    rows, width = queries.shape
    block = rows // clips
    pairs = width // PAIR
    blocks = len(held)
    quarter = width // 4
    big = pltpu.VMEM((rows, width), F32)
    outs = pl.pallas_call(
        functools.partial(forward_kernel, clips, blocks, min(block, 256)),
        in_specs=[SMEM] + [VMEM] * (1 + blocks + 7) + [HBM] * 2,
        out_specs=[VMEM] * 5 + [HBM] * 8,
        out_shape=[
            big,
            jax.ShapeDtypeStruct((clips, pairs, 2, block), F32),
            big,
            big,
            jax.ShapeDtypeStruct((8, width), F32),
        ]
        + [pltpu.HBM((NEAR_BLOCKS, quarter, width), BF)] * 4
        + [pltpu.HBM((2 * quarter, width), BF)] * 2
        + [pltpu.HBM((FAR_BLOCKS, 2 * quarter, width), BF)] * 2,
        scratch_shapes=[
            pltpu.VMEM((rows, width), BF), pltpu.VMEM((width, rows), BF),
            pltpu.VMEM((OWNERS, width // OWNERS, rows), F32), pltpu.VMEM((2, 8, width // 8, rows), BF),
            pltpu.VMEM((FF_STEPS, width, width), BF), pltpu.VMEM((FF_STEPS, width, width), BF),
            pltpu.VMEM((2, 2, 4, quarter, width), BF),
            pltpu.SemaphoreType.DMA((FF_STEPS, 2)), pltpu.SemaphoreType.DMA((2, 2, 4)),
        ],
        compiler_params=params(30),
        cost_estimate=cost(40),
        name="forward",
    )(table, queries, *held, embedded, *vectors, cot, w_out, in_hbm(w_up), in_hbm(w_down))
    return outs[:5], outs[5:9], outs[9:11], outs[11:]


def branch_kernel(
    table_ref, att_ref, emb_ref, result_ref, grad_normed_ref, cot_ref, w_out_ref, bias_out_ref, gain_ref, bias_down_ref,
    output_ref, grad_after_ref, grad_att_ref, dots_ref, small_ref, here_ref, there_ref, slots,
):
    rows, width = emb_ref.shape
    place_blocks(table_ref, jnp.transpose(att_ref[...], (1, 0)), slots)
    output_ref[...] = (result_ref[...] + flat(bias_down_ref)).astype(BF)
    cot = cot_ref[...].astype(F32)
    grad_rows = grad_normed_ref[...]
    unit_rows, inverse_rows = normalize(after_attention(att_ref, emb_ref, w_out_ref, bias_out_ref))
    grad_after = cot + norm_backward(grad_rows, unit_rows, inverse_rows, flat(gain_ref))
    grad_after_ref[...] = grad_after
    branch = grad_after.astype(BF)
    grad_att = dot(branch, w_out_ref[...], NT).astype(BF)
    grad_att_ref[...] = grad_att
    grad_out = dot(slots[...].reshape(width, rows).astype(BF), branch).astype(BF)
    here_ref[...] = grad_out[: width // 2]
    there_ref[...] = grad_out[width // 2 :]
    small_ref[...] = jnp.concatenate(
        [
            total(grad_rows * unit_rows), total(grad_rows), total(branch.astype(F32)), total(cot),
            jnp.zeros((4, width), F32),
        ],
        0,
    )
    product = jnp.transpose(grad_att.astype(F32) * att_ref[...], (1, 0))
    for head in range(width // HEAD_DIM):
        dots_ref[head // 2, head % 2 : head % 2 + 1, :] = total(product[head * HEAD_DIM : (head + 1) * HEAD_DIM])


def branch(table, attended, embedded, result, grad_normed, cot, w_out, bias_out, gain, bias_down):
    rows, width = embedded.shape
    outs = pl.pallas_call(
        branch_kernel,
        in_specs=[SMEM] + [VMEM] * 9,
        out_specs=[VMEM] * 7,
        out_shape=[
            jax.ShapeDtypeStruct((rows, width), BF),
            jax.ShapeDtypeStruct((rows, width), F32),
            jax.ShapeDtypeStruct((rows, width), BF),
            jax.ShapeDtypeStruct((width // PAIR, 2, rows), F32),
            jax.ShapeDtypeStruct((8, width), F32),
            *[jax.ShapeDtypeStruct((width // 2, width), BF)] * 2,
        ],
        scratch_shapes=[pltpu.VMEM((OWNERS, width // OWNERS, rows), F32)],
        compiler_params=params(24),
        cost_estimate=cost(5),
        name="branch",
    )(table, attended, embedded, result, grad_normed, cot, w_out, bias_out, gain, bias_down)
    return outs


def attend_back_kernel(clips, tile, q_ref, grad_ref, log_ref, dots_ref, *refs):
    blocks = (len(refs) - 1) // 2
    held_refs, dq_ref, out_refs = refs[:blocks], refs[blocks], refs[blocks + 1 :]
    rows, width = q_ref.shape
    pairs = width // PAIR
    size = rows // clips
    low_half = lax.broadcasted_iota(jnp.int32, (1, PAIR), 1) < HEAD_DIM
    zero = jnp.zeros((), BF)
    pick = lambda x, half: jnp.where(low_half, x, zero) if half == 0 else jnp.where(low_half, zero, x)
    items = [(block, at, half) for block in range(blocks) for at in range(0, size, tile) for half in range(2)]

    def one(clip, pair, rows_at, lanes):
        queries, grads = q_ref[rows_at, lanes(0)], grad_ref[rows_at, lanes(0)]
        dots = [dots_ref[pair, half : half + 1, rows_at] for half in range(2)]
        logs = [log_ref[clip, pair, half : half + 1, :] for half in range(2)]

        def products(block, at, half):
            ref = held_refs[block].at[rows_at, :]
            keys = pick(ref[at : at + tile, lanes(0)], half)
            values = pick(ref[at : at + tile, lanes(pairs)], half)
            return keys, dot(keys, queries, NT), dot(values, grads, NT)

        ahead = products(*items[0])
        dq_t = jnp.zeros((PAIR, size), F32)
        for i, (block, at, half) in enumerate(items):
            own_keys, scores, grad_probs = ahead
            if i + 1 < len(items):
                ahead = products(*items[i + 1])
            probs = jnp.exp(scores - logs[half])
            grad_scores = (probs * (grad_probs - dots[half])).astype(BF)
            if half == 0:
                dkeys, dvalues = [], []
            dvalues.append(dot(probs.astype(BF), grads))
            dkeys.append(dot(grad_scores, queries))
            dq_t += dot(own_keys, grad_scores, TN)
            if half == 1:
                for j, pair_of in enumerate((dkeys, dvalues)):
                    ref = out_refs[block].at[j, rows_at, :]
                    ref[at : at + tile, lanes(0)] = jnp.where(low_half, *pair_of).astype(ref.dtype)
        dq_ref[rows_at, lanes(0)] = (jnp.transpose(dq_t, (1, 0)) * SCORE_SCALE).astype(BF)

    pair_loop(clips, pairs, size, one)


def attend_back(queries, grads, logs, dots, held, clips):
    rows, width = queries.shape
    blocks = len(held)
    return pl.pallas_call(
        functools.partial(attend_back_kernel, clips, min(rows // clips, 256)),
        in_specs=[VMEM] * (4 + blocks),
        out_specs=[VMEM] * (1 + blocks),
        out_shape=[jax.ShapeDtypeStruct((rows, width), BF), jax.ShapeDtypeStruct((2, rows, width), F32)]
        + [jax.ShapeDtypeStruct((2, rows, width), BF)] * (blocks - 1),
        compiler_params=params(16),
        cost_estimate=cost(17),
        name="attend_back",
    )(queries, grads, logs, dots, *held)


def last_kernel(
    parts, table_ref, normed_t_ref, dq_ref, w_ref, emb_ref, grad_after_ref, order_ref, mask_ref, gain_ref, small_ref,
    bias_up_ref, *refs,
):
    grad_refs, tubes_ref, out_refs, (slots, extra_slots) = refs[:parts], refs[parts], refs[parts + 1 : parts + 5], refs[parts + 5 :]
    rows, width = emb_ref.shape
    store = lambda at, array: store_quarters([ref.at[:, at : at + array.shape[1]] for ref in out_refs], array)
    sums, grad_rows = [], 0.0
    for part in range(3):
        if part == 0:
            packed = dq_ref[...]
        else:
            packed = add([ref[part - 1] for ref in grad_refs]).astype(BF)
        sums.append(total(packed.astype(F32)))
        store(part * width, dot(normed_t_ref[...], packed))
        grad_rows += dot(packed, w_ref[:, part * width : (part + 1) * width], NT)
    grad_after = grad_after_ref[...]
    unit, inverse = normalize(emb_ref[...])
    grad = grad_after + norm_backward(grad_rows, unit, inverse, flat(gain_ref))
    kept = jnp.where(wide_mask(mask_ref, width), 0.0, grad)
    tubes_ref[...] = kept
    place_blocks(table_ref, jnp.transpose(grad, (1, 0)), slots)
    length = out_refs[0].shape[1] - 3 * width - EXTRA
    store(3 * width, dot(slots[...].reshape(width, rows).astype(BF), one_hot(order_ref, length)))
    stacked = jnp.concatenate(
        [
            total(grad - kept), total(grad_rows * unit), total(grad_rows), sums[0], sums[2],
            small_ref[0:4, :], bias_up_ref[0:FF_STEPS, :], jnp.zeros((EXTRA - 9 - FF_STEPS, width), F32),
        ],
        0,
    )
    extra = jnp.transpose(stacked, (1, 0))
    lanes = lax.broadcasted_iota(jnp.int32, (1, EXTRA), 1)
    size = width // OWNERS
    for feed in range(FF_STEPS):
        column = jnp.broadcast_to(extra[:, 9 + feed : 10 + feed], extra.shape)
        for i in range(OWNERS // FF_STEPS):
            owner = feed * (OWNERS // FF_STEPS) + i
            tile = extra[owner * size : (owner + 1) * size]
            for k in range(4):
                tile = jnp.where(lanes == 9 + k, column[(i * 4 + k) * size : (i * 4 + k + 1) * size], tile)
            extra_slots[table_ref[SLOT + owner]] = tile
    store(3 * width + length, extra_slots[...].reshape(width, EXTRA))


def last(table, normed_t, dq, w_qkv, embedded, grad_after, order, mask, gain, small, bias_up, grads, length):
    rows, width = embedded.shape
    outs = pl.pallas_call(
        functools.partial(last_kernel, len(grads)),
        in_specs=[SMEM] + [VMEM] * (10 + len(grads)),
        out_specs=[VMEM] * 5,
        out_shape=[jax.ShapeDtypeStruct((rows, width), F32)]
        + [jax.ShapeDtypeStruct((width // 4, 3 * width + length + EXTRA), BF)] * 4,
        scratch_shapes=[
            pltpu.VMEM((OWNERS, width // OWNERS, rows), F32),
            pltpu.VMEM((OWNERS, width // OWNERS, EXTRA), F32),
        ],
        compiler_params=params(24),
        cost_estimate=cost(8),
        name="last",
    )(table, normed_t, dq, w_qkv, embedded, grad_after, order, mask, gain, small, bias_up, *grads)
    return outs[0], outs[1:]


def swap(array, stage):
    if stage == 0:
        return lax.ppermute(array, "blk", [(0, 1), (1, 0)])
    if stage < 3:
        apart = lambda core: 2 if core == (stage == 2) else 4
        return lax.ppermute(array, ALL, [(i, i ^ apart(i % 2 == 1)) for i in range(OWNERS)])
    step = 4 << (stage - 3)
    return lax.ppermute(array, "dp", [(i, i ^ step) for i in range(OWNERS // 2)])


def crossed(parts):
    ahead, later = swap(parts[3], 0), swap(parts[2], 0)
    return [parts[0], later], [parts[1], ahead]


def cut(terms, at):
    halves = [jnp.split(x, 2, at) for x in terms]
    return [x[0] for x in halves], [x[1] for x in halves]


def join(groups):
    sums = [add(terms).astype(BF) for terms in groups]
    return jnp.concatenate([x.reshape(-1, x.shape[-1]) for x in sums], 0)


def part(received, groups):
    at = 0
    for terms in groups:
        shape = terms[0].shape
        size = math.prod(shape[:-1])
        terms.append(received[at : at + size].reshape(shape))
        at += size


def order_after(values, arrays):
    held = lax.optimization_barrier((tuple(values), tuple(arrays)))
    return held[0], held[1]


def natural(parts):
    columns = parts[0].shape[-1]
    array = jnp.stack([part.reshape(2, 4, -1, columns) for part in parts])
    array = array.reshape((2, 2, 2, 2, 2, -1, columns))
    return array.transpose((4, 3, 2, 1, 0, 5, 6)).reshape(-1, columns)


def body(
    paired,
    tubes, tube_mask, tube_order, cotangent, mask_token, pos_table, ln1_gain, ln1_bias, w_qkv, bias_q, bias_v,
    w_out, bias_out, ln2_gain, ln2_bias, w_up, bias_up, w_down, bias_down,
):
    clips, block, width = tubes.shape
    rows = clips * block
    blocks = lax.axis_size("blk")
    length = block * blocks
    owners = jnp.arange(OWNERS, dtype=jnp.int32)
    core = lax.axis_index("blk") if paired else 0
    me = lax.axis_index("dp") * 2 + core if paired else 0
    apart = jnp.bitwise_xor(owners, me)
    bit = lambda b: (apart >> b) & 1
    turned = jnp.bitwise_xor(core, bit(0)) if paired else 0
    first, second = jnp.where(turned == 0, bit(1), bit(2)), jnp.where(turned == 0, bit(2), bit(1))
    within = bit(0) * 4 + first * 2 + second
    layer = bit(3) * 2 + bit(4)
    table = jnp.concatenate([within * 4 + layer, within[:8], layer[::8]])

    order, mask = tube_order.reshape(1, rows), tube_mask.reshape(1, rows)
    cot = cotangent.reshape(rows, width)
    embedded, normed_t, queries, kv = embed(
        table, order, mask, pos_table, tubes.reshape(rows, width), (mask_token, ln1_gain, ln1_bias, bias_q, bias_v), w_qkv
    )
    held = [kv] + [
        lax.ppermute(kv, "blk", [(i, (i + s) % blocks) for i in range(blocks)]) for s in range(1, blocks)
    ]
    (attended, logs, result, grad_normed, bias_up_grad), near_parts, middle_parts, far_parts = forward(
        table, queries, held, embedded, (bias_out, ln2_gain, ln2_bias, bias_up), cot, w_out, w_up, w_down, clips
    )
    if paired:
        ahead, far_got, middle_got = swap(near_parts[3], 0), swap(far_parts[1], 0), swap(middle_parts[1], 0)
    output, grad_after, grad_att, dots, small, *out_parts = branch(
        table, attended, embedded, result, grad_normed, cot, w_out, bias_out, ln2_gain, bias_down
    )
    if paired:
        (grad_att,), (ahead, far_got, middle_got) = order_after((grad_att,), (ahead, far_got, middle_got))
        near = [near_parts[0], swap(near_parts[2], 0)]
        far, far_go = cut([far_parts[0], far_got], 1)
        middle, middle_go = cut([middle_parts[0], middle_got], 0)
        sent = [add(terms).astype(BF) for terms in ([near_parts[1], ahead], far_go, middle_go)]
        (grad_att,), sent = order_after((grad_att,), sent)
        near.append(swap(sent[0], 1))
        far.append(swap(sent[1], 3))
        middle.append(swap(sent[2], 1))
        out = [x.reshape(2, 2, -1, width) for x in (out_parts[0], swap(out_parts[1], 0))]
    home = lambda x, s: lax.ppermute(x, "blk", [((i + s) % blocks, i) for i in range(blocks)])
    dq, own, *away = attend_back(queries, grad_att, logs, dots, held, clips)
    if paired:
        away, (near[-1], far[-1]) = order_after(away, (near[-1], far[-1]))
        near, near_go = cut([x.reshape(NEAR_BLOCKS, 2, -1, width) for x in near], 1)
        out, out_go = cut(out, 1)
        near_got = swap(join([near_go, out_go]), 2)
        far, far_go = cut(far, 1)
        far_got = swap(join([far_go]), 4)
    grads = [home(x, s + 1) for s, x in enumerate(away)]
    grad_tubes, late_parts = last(
        table, normed_t, dq, w_qkv, embedded, grad_after, order, mask, ln1_gain, small, bias_up_grad,
        [own, *grads], length,
    )
    if paired:
        late_parts, (near_got, far_got, middle[-1]) = order_after(late_parts, (near_got, far_got, middle[-1]))
        late, late_go = crossed(late_parts)
        part(near_got, (near, out))
        part(far_got, (far,))
        near = [x.reshape(NEAR_BLOCKS, -1, width) for x in near]
        down, up = [x[:FF_STEPS].reshape(-1, width) for x in near], [x[FF_STEPS] for x in near]
        middle, middle_go = cut(middle, 0)
        middle.append(swap(add(middle_go).astype(BF), 2))
        late.append(swap(add(late_go).astype(BF), 1))
        far, far_go = cut(far, 1)
        out, out_go = cut(out, 0)
        part(swap(join([far_go, out_go]), 1), (far, out))
        out = [x.reshape(-1, width) for x in out]
        for stage in (3, 4):
            sums = [cut(terms, 0) for terms in (down, up, middle, out)]
            down, up, middle, out = (keep for keep, _ in sums)
            part(swap(join([go for _, go in sums]), stage), (down, up, middle, out))
        far, far_go = cut(far, 1)
        part(swap(join([far_go]), 2), (far,))
        for stage in (2, 3, 4):
            late, go = cut(late, 0)
            late.append(swap(add(go).astype(BF), stage))
        grad_w_down, grad_w_out = add(down), add(out)
        grad_w_up = jnp.concatenate([add(up), add(middle), *add(far)], 1)
        late = add(late)
    else:
        spread = lambda array: lax.psum_scatter(array.astype(F32), ALL, scatter_dimension=0, tiled=True)
        quarters = lambda halves: [x for half in halves for x in jnp.split(half, 2, 0)]
        down = [x[:FF_STEPS].reshape(4, 2, -1, width).swapaxes(0, 1) for x in near_parts]
        far = [x.reshape(FAR_BLOCKS, 4, 2, 2, -1, width).transpose((2, 3, 1, 4, 0, 5)) for x in far_parts]
        far = [x.reshape(-1, FAR_BLOCKS * width) for half in far for x in half]
        up = [jnp.concatenate([x[FF_STEPS], y, z], 1) for x, y, z in zip(near_parts, quarters(middle_parts), far)]
        grad_w_down, grad_w_up = spread(natural(down)), spread(natural(up))
        grad_w_out, late = spread(natural(quarters(out_parts))), spread(natural(late_parts))
    grad_w_qkv, grad_pos, extra = jnp.split(late, [3 * width, 3 * width + length], 1)
    grad_bias_up = extra[:, 9:13].T.reshape(-1) if paired else spread(bias_up_grad[:FF_STEPS].reshape(-1))
    mask_grad, gain_one, shift_one, grad_bias_q, grad_bias_v, gain_two, shift_two, grad_bias_out, grad_bias_down = (
        extra[:, i] for i in range(9)
    )
    return (
        output.reshape(clips, block, width),
        grad_tubes.reshape(clips, block, width),
        mask_grad,
        grad_pos.T,
        gain_one,
        shift_one,
        grad_w_qkv,
        grad_bias_q,
        grad_bias_v,
        grad_w_out,
        grad_bias_out,
        gain_two,
        shift_two,
        grad_w_up,
        grad_bias_up,
        grad_w_down,
        grad_bias_down,
    )


def solution(mesh):
    split = P("dp", "blk", None)
    flat = P("dp", "blk")
    in_specs = (split, flat, flat, split) + (P(),) * 15
    one, two = P(ALL), P(ALL, None)
    out_specs = (split, split, one, P(None, ALL), one, one, two, one, one, two, one, one, one, two, one, two, one)
    paired = mesh.shape["blk"] == 2 and mesh.shape["dp"] == OWNERS // 2
    return jax.shard_map(
        functools.partial(body, paired), mesh=mesh, in_specs=in_specs, out_specs=out_specs, check_vma=False
    )
```

```python
import functools
import math

import jax
import jax.numpy as jnp
from jax import lax
from jax.experimental import pallas as pl
from jax.experimental.pallas import tpu as pltpu
from jax.sharding import PartitionSpec as P

HEADS = 12
HEAD_DIM = 64
PAIR = 2 * HEAD_DIM
EPSILON = 1e-06
SCORE_SCALE = 0.125
OWNERS = 32
EXTRA = 128
BF = jnp.bfloat16
F32 = jnp.float32
ALL = ("dp", "blk")
MIB = 1 << 20

NN = (((1,), (0,)), ((), ()))
NT = (((1,), (1,)), ((), ()))
TN = (((0,), (0,)), ((), ()))


def dot(left, right, dims=NN):
    return lax.dot_general(left, right, dims, preferred_element_type=F32)


def cost(micros):
    return pl.CostEstimate(flops=int(micros * 1e9), bytes_accessed=int(micros * 1e6), transcendentals=0)


def params(mib):
    return pltpu.CompilerParams(vmem_limit_bytes=mib * MIB)


def normalize(rows):
    centered = rows - jnp.mean(rows, -1, keepdims=True)
    inverse = lax.rsqrt(jnp.mean(centered * centered, -1, keepdims=True) + EPSILON)
    return centered * inverse, inverse


def norm_backward(grad, unit, inverse, gain):
    scaled = grad * gain
    return inverse * (
        scaled
        - jnp.mean(scaled, -1, keepdims=True)
        - unit * jnp.mean(scaled * unit, -1, keepdims=True)
    )


def lane_columns(row):
    return jnp.transpose(jnp.broadcast_to(row, (128, row.shape[1])), (1, 0))


def store_quarters(refs, array):
    quarter = array.shape[0] // 4
    for i, ref in enumerate(refs):
        ref[...] = array[i * quarter : (i + 1) * quarter].astype(BF)


SLOT, WITHIN, LAYER = 0, OWNERS, OWNERS + 8


def place_blocks(table_ref, transposed, slots):
    size = transposed.shape[0] // OWNERS
    for owner in range(OWNERS):
        slots[table_ref[SLOT + owner]] = transposed[owner * size : (owner + 1) * size]


def flat(ref):
    return ref[...].reshape(1, -1)


def add(terms):
    return functools.reduce(jnp.add, [x.astype(F32) for x in terms])


def total(rows):
    return jnp.sum(rows, 0, keepdims=True)


VMEM = pl.BlockSpec(memory_space=pltpu.VMEM)
SMEM = pl.BlockSpec(memory_space=pltpu.SMEM)
ANY = pl.BlockSpec(memory_space=pl.ANY)
HBM = pl.BlockSpec(memory_space=pltpu.HBM)


def in_hbm(array):
    return pltpu.with_memory_space_constraint(array, pltpu.HBM)


def one_hot(order_ref, length):
    order = lane_columns(order_ref[...].astype(F32))
    lanes = lax.broadcasted_iota(jnp.int32, order.shape, 1).astype(F32)
    return jnp.concatenate([jnp.where(order == lanes + at, 1.0, 0.0).astype(BF) for at in range(0, length, 128)], 1)


def wide_mask(mask_ref, width):
    mask = lane_columns(mask_ref[...].astype(F32))
    return jnp.concatenate([mask] * (width // 128), 1) > 0.5


def embed_kernel(table_ref, *refs):
    sources, refs = refs[:10], refs[10:]
    (emb_ref, normed_t_ref, q_ref, kv_ref), refs = refs[:4], refs[4:]
    places, (normed, slots, w, sems) = refs[:9], refs[9:]
    order_ref, mask_ref, positions_ref, tubes_ref, token_ref, gain_ref, shift_ref, bias_q_ref, bias_v_ref = places
    rows, width = tubes_ref.shape
    loads = [pltpu.make_async_copy(source, place, sems.at[i]) for i, (source, place) in enumerate(zip(sources, places))]
    w_ref = sources[9]
    loads += [
        pltpu.make_async_copy(w_ref.at[:, pl.ds(part * width, width)], w.at[part], sems.at[9 + part]) for part in range(3)
    ]
    for load in loads:
        load.start()
    loads[0].wait()
    hot = one_hot(order_ref, positions_ref.shape[0])
    for load in loads[1:9]:
        load.wait()
    masks = wide_mask(mask_ref, width)
    embedded = jnp.where(masks, flat(token_ref), tubes_ref[...].astype(F32)) + dot(hot, positions_ref[...])
    emb_ref[...] = embedded
    unit, _ = normalize(embedded)
    normed_rows = unit * flat(gain_ref) + flat(shift_ref)
    normed[...] = normed_rows.astype(BF)
    for load in loads[9:]:
        load.wait()
    kv_ref[:, :width] = dot(normed[...], w[1]).astype(BF)
    kv_ref[:, width:] = (dot(normed[...], w[2]) + flat(bias_v_ref)).astype(BF)
    queries = (dot(normed[...], w[0]) + flat(bias_q_ref)).astype(BF)
    q_ref[...] = (queries.astype(F32) * SCORE_SCALE).astype(BF)
    place_blocks(table_ref, jnp.transpose(normed_rows, (1, 0)), slots)
    normed_t_ref[...] = slots[...].reshape(width, rows).astype(BF)


def embed(table, order, mask, positions, tubes, vectors, w_qkv):
    rows, width = tubes.shape
    sources = (order, mask, positions, tubes, *vectors)
    return pl.pallas_call(
        embed_kernel,
        in_specs=[SMEM] + [HBM] * 10,
        out_specs=[VMEM] * 4,
        out_shape=[
            jax.ShapeDtypeStruct((rows, width), F32),
            jax.ShapeDtypeStruct((width, rows), BF),
            jax.ShapeDtypeStruct((rows, width), BF),
            jax.ShapeDtypeStruct((rows, 2 * width), BF),
        ],
        scratch_shapes=[pltpu.VMEM(x.shape, x.dtype) for x in sources]
        + [
            pltpu.VMEM((rows, width), BF),
            pltpu.VMEM((OWNERS, width // OWNERS, rows), F32),
            pltpu.VMEM((3, width, width), BF),
            pltpu.SemaphoreType.DMA((12,)),
        ],
        compiler_params=params(24),
        cost_estimate=cost(6),
        name="embed",
    )(table, *[in_hbm(x) for x in (*sources, w_qkv)])


def attend_pair(queries_ref, keys, values, tile, out_ref, log_ref):
    low_half = lax.broadcasted_iota(jnp.int32, (1, PAIR), 1) < HEAD_DIM
    one, zero = jnp.ones((), BF), jnp.zeros((), BF)
    value_halves = [jnp.where(low_half, values, one), jnp.where(low_half, one, values)]
    items = [(at, half) for at in range(0, queries_ref.shape[0], tile) for half in range(2)]

    def score(at, half):
        queries = queries_ref[at : at + tile, :]
        own = jnp.where(low_half, queries, zero) if half == 0 else jnp.where(low_half, zero, queries)
        return dot(own, keys, NT)

    ahead = score(*items[0])
    for i, (at, half) in enumerate(items):
        scores = ahead
        if i + 1 < len(items):
            ahead = score(*items[i + 1])
        if half == 0:
            tops, mixed = [], []
        top = jnp.max(scores, -1, keepdims=True)
        weights = jnp.exp(scores - top).astype(BF)
        tops.append(top)
        mixed.append(dot(weights, value_halves[half]))
        if half == 0:
            continue
        sums = pltpu.roll(jnp.where(low_half, mixed[1], mixed[0]), HEAD_DIM, 1)
        out_ref[at : at + tile, :] = jnp.where(low_half, mixed[0], mixed[1]) / sums
        logs = jnp.where(low_half, tops[0], tops[1]) + jnp.log(sums)
        logs = jnp.transpose(logs, (1, 0))
        log_ref[0:1, at : at + tile] = logs[0:1]
        log_ref[1:2, at : at + tile] = logs[HEAD_DIM : HEAD_DIM + 1]


def gelu_terms(x):
    bell = jnp.exp(x * x * -0.5)
    t = 1.0 / (1.0 + jnp.abs(x) * (0.3275911 * math.sqrt(0.5)))
    a1, a2, a3, a4, a5 = (0.5 * a for a in (0.254829592, -0.284496736, 1.421413741, -1.453152027, 1.061405429))
    tail = t * (a1 + t * (a2 + t * (a3 + t * (a4 + t * a5)))) * bell
    cdf = jnp.where(x >= 0.0, 1.0 - tail, tail)
    return x * cdf, cdf + x * bell * (1.0 / math.sqrt(2.0 * math.pi))


FF_STEPS = 4
NEAR_BLOCKS, FAR_BLOCKS = FF_STEPS + 1, FF_STEPS - 2


def pair_loop(clips, pairs, block, work):
    def step(i, carry):
        clip, pair = lax.div(i, pairs), lax.rem(i, pairs)
        at = pl.ds(pl.multiple_of(clip * block, block), block)
        work(clip, pair, at, lambda off: pl.ds(pl.multiple_of((pair + off) * PAIR, PAIR), PAIR))
        return carry

    lax.fori_loop(0, clips * pairs, step, 0)


def after_attention(att_ref, emb_ref, w_ref, bias_ref):
    return emb_ref[...] + dot(att_ref[...].astype(BF), w_ref[...]) + flat(bias_ref)


def forward_kernel(clips, blocks, tile, table_ref, q_ref, *refs):
    held_refs = refs[:blocks]
    (
        emb_ref, bias_out_ref, gain_ref, shift_ref, bias_in_ref, cot_ref, w_out_ref, w_up_ref, w_down_ref,
        att, log_ref, result, grad_normed, bias_up_ref,
    ) = refs[blocks : 14 + blocks]
    near_refs, middle_refs, far_refs = (refs[14 + blocks :][i:j] for i, j in ((0, 4), (4, 6), (6, 8)))
    normed, normed_t, slots, act_slots, act_all, pre_all, w_up, w_down, stage, in_sems, out_sems = refs[22 + blocks :]
    rows, width = emb_ref.shape
    pairs = width // PAIR
    quarter = width // 4
    loads = []
    for f in range(FF_STEPS):
        at = pl.ds(f * width, width)
        loads.append(
            [
                pltpu.make_async_copy(w_up_ref.at[:, at], w_up.at[f], in_sems.at[f, 0]),
                pltpu.make_async_copy(w_down_ref.at[at, :], w_down.at[f], in_sems.at[f, 1]),
            ]
        )
        for load in loads[f]:
            load.start()

    def attend_one(clip, pair, at, lanes):
        keys = jnp.concatenate([ref[at, lanes(0)] for ref in held_refs], 0)
        values = jnp.concatenate([ref[at, lanes(pairs)] for ref in held_refs], 0)
        attend_pair(q_ref.at[at, lanes(0)], keys, values, tile, att.at[at, lanes(0)], log_ref.at[clip, pair])

    pair_loop(clips, pairs, rows // clips, attend_one)

    after = after_attention(att, emb_ref, w_out_ref, bias_out_ref)
    unit_rows, inverse_rows = normalize(after)
    normed_rows = unit_rows * flat(gain_ref) + flat(shift_ref)
    normed[...] = normed_rows.astype(BF)
    result[...] = after
    place_blocks(table_ref, jnp.transpose(normed_rows, (1, 0)), slots)
    normed_t[...] = slots[...].reshape(width, rows).astype(BF)

    stores = {}

    def store(f, kind, array):
        for old in stores.pop((kind, f % 2), ()):
            old.wait()
        copies = []
        parts = [array[i * quarter : (i + 1) * quarter] for i in range(4)]
        if kind == 0:
            targets = [ref.at[table_ref[LAYER + f]] for ref in near_refs]
        elif f == 0:
            targets = [ref.at[FF_STEPS] for ref in near_refs]
        elif f == 1:
            targets = [middle_refs[i // 2].at[pl.ds(i % 2 * quarter, quarter)] for i in range(4)]
        else:
            targets = [far_refs[i // 2].at[f - 2, pl.ds(i % 2 * quarter, quarter)] for i in range(4)]
            owner = width // OWNERS
            by_z = [i * 16 + xy * 4 + z for i in range(2) for z in range(4) for xy in range(4)]
            parts = [
                jnp.concatenate([array[slot * owner : (slot + 1) * owner] for slot in by_z[i * 8 : i * 8 + 8]], 0)
                for i in range(4)
            ]
        for i, (part, target) in enumerate(zip(parts, targets)):
            place = stage.at[kind, f % 2, i]
            place[...] = part.astype(BF)
            copies.append(pltpu.make_async_copy(place, target, out_sems.at[kind, f % 2, i]))
            copies[-1].start()
        stores[kind, f % 2] = copies

    halves = 2
    span = rows // halves
    own = OWNERS // FF_STEPS

    def products(f, h):
        rows_at = slice(h * span, (h + 1) * span)
        bias = flat(bias_in_ref)[:, f * width : (f + 1) * width]
        return dot(normed[rows_at, :], w_up[f]) + bias, dot(cot_ref[rows_at, :], w_down[f], NT)

    def activate(f, h, pre_act, grad_active):
        active, slope = gelu_terms(pre_act)
        grad_pre = (grad_active * slope).astype(BF)
        rows_at = slice(h * span, (h + 1) * span)
        act_all[f % 2, rows_at, :] = active.astype(BF)
        pre_all[f % 2, rows_at, :] = grad_pre
        active_t = jnp.transpose(active, (1, 0)).astype(BF)
        for k in range(own):
            act_slots[f % 2, table_ref[WITHIN + k], :, rows_at] = active_t[k * (width // own) : (k + 1) * (width // own)]

    def tasks(f):
        held = {}

        def add_up(h):
            rows_at = slice(h * span, (h + 1) * span)
            result[rows_at, :] += dot(act_all[f % 2, rows_at, :], w_down[f])
            term = dot(pre_all[f % 2, rows_at, :], w_up[f], NT)
            if f == 0:
                grad_normed[rows_at, :] = term
            else:
                grad_normed[rows_at, :] += term

        def grad_part(kind, p):
            at = slice(p * width // 3, (p + 1) * width // 3)
            left = normed_t[at, :] if kind else act_slots[f % 2].reshape(width, rows)[at, :]
            right = pre_all[f % 2] if kind else cot_ref[...]
            held[kind, p] = dot(left, right)
            if p == 2:
                store(f, kind, jnp.concatenate([held[kind, i] for i in range(3)], 0))

        def bias_sum():
            bias_up_ref[f : f + 1, :] = total(pre_all[f % 2].astype(F32))

        out = [functools.partial(add_up, h) for h in range(halves)]
        out += [functools.partial(grad_part, kind, p) for kind in (1, 0) for p in range(3)]
        return out + [bias_sum]

    waiting = []
    for f in range(FF_STEPS):
        for load in loads[f]:
            load.wait()
        each = -(-len(waiting) // halves)
        ahead = products(f, 0)
        for h in range(halves):
            now = ahead
            if h + 1 < halves:
                ahead = products(f, h + 1)
            batch, waiting = waiting[:each], waiting[each:]
            for task in batch[: len(batch) // 2]:
                task()
            activate(f, h, *now)
            for task in batch[len(batch) // 2 :]:
                task()
        waiting = tasks(f)
    for task in waiting:
        task()
    bias_up_ref[FF_STEPS:, :] = jnp.zeros((8 - FF_STEPS, width), F32)
    for copies in stores.values():
        for copy in copies:
            copy.wait()


def forward(table, queries, held, embedded, vectors, cot, w_out, w_up, w_down, clips):
    rows, width = queries.shape
    block = rows // clips
    pairs = width // PAIR
    blocks = len(held)
    quarter = width // 4
    big = pltpu.VMEM((rows, width), F32)
    outs = pl.pallas_call(
        functools.partial(forward_kernel, clips, blocks, min(block, 256)),
        in_specs=[SMEM] + [VMEM] * (1 + blocks + 7) + [HBM] * 2,
        out_specs=[VMEM] * 5 + [HBM] * 8,
        out_shape=[
            big,
            jax.ShapeDtypeStruct((clips, pairs, 2, block), F32),
            big,
            big,
            jax.ShapeDtypeStruct((8, width), F32),
        ]
        + [pltpu.HBM((NEAR_BLOCKS, quarter, width), BF)] * 4
        + [pltpu.HBM((2 * quarter, width), BF)] * 2
        + [pltpu.HBM((FAR_BLOCKS, 2 * quarter, width), BF)] * 2,
        scratch_shapes=[
            pltpu.VMEM((rows, width), BF), pltpu.VMEM((width, rows), BF),
            pltpu.VMEM((OWNERS, width // OWNERS, rows), F32), pltpu.VMEM((2, 8, width // 8, rows), BF),
            pltpu.VMEM((2, rows, width), BF), pltpu.VMEM((2, rows, width), BF),
            pltpu.VMEM((FF_STEPS, width, width), BF), pltpu.VMEM((FF_STEPS, width, width), BF),
            pltpu.VMEM((2, 2, 4, quarter, width), BF),
            pltpu.SemaphoreType.DMA((FF_STEPS, 2)), pltpu.SemaphoreType.DMA((2, 2, 4)),
        ],
        compiler_params=params(32),
        cost_estimate=cost(40),
        name="forward",
    )(table, queries, *held, embedded, *vectors, cot, w_out, in_hbm(w_up), in_hbm(w_down))
    return outs[:5], outs[5:9], outs[9:11], outs[11:]


def branch_kernel(
    table_ref, att_ref, emb_ref, result_ref, grad_normed_ref, cot_ref, w_out_ref, bias_out_ref, gain_ref, bias_down_ref,
    output_ref, grad_after_ref, grad_att_ref, dots_ref, small_ref, here_ref, there_ref, slots,
):
    rows, width = emb_ref.shape
    place_blocks(table_ref, jnp.transpose(att_ref[...], (1, 0)), slots)
    output_ref[...] = (result_ref[...] + flat(bias_down_ref)).astype(BF)
    cot = cot_ref[...].astype(F32)
    grad_rows = grad_normed_ref[...]
    unit_rows, inverse_rows = normalize(after_attention(att_ref, emb_ref, w_out_ref, bias_out_ref))
    grad_after = cot + norm_backward(grad_rows, unit_rows, inverse_rows, flat(gain_ref))
    grad_after_ref[...] = grad_after
    branch = grad_after.astype(BF)
    grad_att = dot(branch, w_out_ref[...], NT).astype(BF)
    grad_att_ref[...] = grad_att
    grad_out = dot(slots[...].reshape(width, rows).astype(BF), branch).astype(BF)
    here_ref[...] = grad_out[: width // 2]
    there_ref[...] = grad_out[width // 2 :]
    small_ref[...] = jnp.concatenate(
        [
            total(grad_rows * unit_rows), total(grad_rows), total(branch.astype(F32)), total(cot),
            jnp.zeros((4, width), F32),
        ],
        0,
    )
    product = jnp.transpose(grad_att.astype(F32) * att_ref[...], (1, 0))
    for head in range(width // HEAD_DIM):
        dots_ref[head // 2, head % 2 : head % 2 + 1, :] = total(product[head * HEAD_DIM : (head + 1) * HEAD_DIM])


def branch(table, attended, embedded, result, grad_normed, cot, w_out, bias_out, gain, bias_down):
    rows, width = embedded.shape
    outs = pl.pallas_call(
        branch_kernel,
        in_specs=[SMEM] + [VMEM] * 9,
        out_specs=[VMEM] * 7,
        out_shape=[
            jax.ShapeDtypeStruct((rows, width), BF),
            jax.ShapeDtypeStruct((rows, width), F32),
            jax.ShapeDtypeStruct((rows, width), BF),
            jax.ShapeDtypeStruct((width // PAIR, 2, rows), F32),
            jax.ShapeDtypeStruct((8, width), F32),
            *[jax.ShapeDtypeStruct((width // 2, width), BF)] * 2,
        ],
        scratch_shapes=[pltpu.VMEM((OWNERS, width // OWNERS, rows), F32)],
        compiler_params=params(24),
        cost_estimate=cost(5),
        name="branch",
    )(table, attended, embedded, result, grad_normed, cot, w_out, bias_out, gain, bias_down)
    return outs


def attend_back_kernel(clips, tile, q_ref, grad_ref, log_ref, dots_ref, *refs):
    blocks = (len(refs) - 1) // 2
    held_refs, dq_ref, out_refs = refs[:blocks], refs[blocks], refs[blocks + 1 :]
    rows, width = q_ref.shape
    pairs = width // PAIR
    size = rows // clips
    low_half = lax.broadcasted_iota(jnp.int32, (1, PAIR), 1) < HEAD_DIM
    zero = jnp.zeros((), BF)
    pick = lambda x, half: jnp.where(low_half, x, zero) if half == 0 else jnp.where(low_half, zero, x)
    items = [(block, at, half) for block in range(blocks) for at in range(0, size, tile) for half in range(2)]

    def one(clip, pair, rows_at, lanes):
        queries, grads = q_ref[rows_at, lanes(0)], grad_ref[rows_at, lanes(0)]
        dots = [dots_ref[pair, half : half + 1, rows_at] for half in range(2)]
        logs = [log_ref[clip, pair, half : half + 1, :] for half in range(2)]

        def products(block, at, half):
            ref = held_refs[block].at[rows_at, :]
            keys = pick(ref[at : at + tile, lanes(0)], half)
            values = pick(ref[at : at + tile, lanes(pairs)], half)
            return keys, dot(keys, queries, NT), dot(values, grads, NT)

        ahead = products(*items[0])
        dq_t = jnp.zeros((PAIR, size), F32)
        for i, (block, at, half) in enumerate(items):
            own_keys, scores, grad_probs = ahead
            if i + 1 < len(items):
                ahead = products(*items[i + 1])
            probs = jnp.exp(scores - logs[half])
            grad_scores = (probs * (grad_probs - dots[half])).astype(BF)
            if half == 0:
                dkeys, dvalues = [], []
            dvalues.append(dot(probs.astype(BF), grads))
            dkeys.append(dot(grad_scores, queries))
            dq_t += dot(own_keys, grad_scores, TN)
            if half == 1:
                for j, pair_of in enumerate((dkeys, dvalues)):
                    ref = out_refs[block].at[j, rows_at, :]
                    ref[at : at + tile, lanes(0)] = jnp.where(low_half, *pair_of).astype(ref.dtype)
        dq_ref[rows_at, lanes(0)] = (jnp.transpose(dq_t, (1, 0)) * SCORE_SCALE).astype(BF)

    pair_loop(clips, pairs, size, one)


def attend_back(queries, grads, logs, dots, held, clips):
    rows, width = queries.shape
    blocks = len(held)
    return pl.pallas_call(
        functools.partial(attend_back_kernel, clips, min(rows // clips, 256)),
        in_specs=[VMEM] * (4 + blocks),
        out_specs=[VMEM] * (1 + blocks),
        out_shape=[jax.ShapeDtypeStruct((rows, width), BF), jax.ShapeDtypeStruct((2, rows, width), F32)]
        + [jax.ShapeDtypeStruct((2, rows, width), BF)] * (blocks - 1),
        compiler_params=params(16),
        cost_estimate=cost(17),
        name="attend_back",
    )(queries, grads, logs, dots, *held)


def last_kernel(
    parts, table_ref, normed_t_ref, dq_ref, w_ref, emb_ref, grad_after_ref, order_ref, mask_ref, gain_ref, small_ref,
    bias_up_ref, *refs,
):
    grad_refs, tubes_ref, out_refs, (slots, extra_slots) = refs[:parts], refs[parts], refs[parts + 1 : parts + 5], refs[parts + 5 :]
    rows, width = emb_ref.shape
    store = lambda at, array: store_quarters([ref.at[:, at : at + array.shape[1]] for ref in out_refs], array)
    sums, grad_rows = [], 0.0
    for part in range(3):
        if part == 0:
            packed = dq_ref[...]
        else:
            packed = add([ref[part - 1] for ref in grad_refs]).astype(BF)
        sums.append(total(packed.astype(F32)))
        store(part * width, dot(normed_t_ref[...], packed))
        grad_rows += dot(packed, w_ref[:, part * width : (part + 1) * width], NT)
    grad_after = grad_after_ref[...]
    unit, inverse = normalize(emb_ref[...])
    grad = grad_after + norm_backward(grad_rows, unit, inverse, flat(gain_ref))
    kept = jnp.where(wide_mask(mask_ref, width), 0.0, grad)
    tubes_ref[...] = kept
    place_blocks(table_ref, jnp.transpose(grad, (1, 0)), slots)
    length = out_refs[0].shape[1] - 3 * width - EXTRA
    store(3 * width, dot(slots[...].reshape(width, rows).astype(BF), one_hot(order_ref, length)))
    stacked = jnp.concatenate(
        [
            total(grad - kept), total(grad_rows * unit), total(grad_rows), sums[0], sums[2],
            small_ref[0:4, :], bias_up_ref[0:FF_STEPS, :], jnp.zeros((EXTRA - 9 - FF_STEPS, width), F32),
        ],
        0,
    )
    extra = jnp.transpose(stacked, (1, 0))
    lanes = lax.broadcasted_iota(jnp.int32, (1, EXTRA), 1)
    size = width // OWNERS
    for feed in range(FF_STEPS):
        column = jnp.broadcast_to(extra[:, 9 + feed : 10 + feed], extra.shape)
        for i in range(OWNERS // FF_STEPS):
            owner = feed * (OWNERS // FF_STEPS) + i
            tile = extra[owner * size : (owner + 1) * size]
            for k in range(4):
                tile = jnp.where(lanes == 9 + k, column[(i * 4 + k) * size : (i * 4 + k + 1) * size], tile)
            extra_slots[table_ref[SLOT + owner]] = tile
    store(3 * width + length, extra_slots[...].reshape(width, EXTRA))


def last(table, normed_t, dq, w_qkv, embedded, grad_after, order, mask, gain, small, bias_up, grads, length):
    rows, width = embedded.shape
    outs = pl.pallas_call(
        functools.partial(last_kernel, len(grads)),
        in_specs=[SMEM] + [VMEM] * (10 + len(grads)),
        out_specs=[VMEM] * 5,
        out_shape=[jax.ShapeDtypeStruct((rows, width), F32)]
        + [jax.ShapeDtypeStruct((width // 4, 3 * width + length + EXTRA), BF)] * 4,
        scratch_shapes=[
            pltpu.VMEM((OWNERS, width // OWNERS, rows), F32),
            pltpu.VMEM((OWNERS, width // OWNERS, EXTRA), F32),
        ],
        compiler_params=params(24),
        cost_estimate=cost(8),
        name="last",
    )(table, normed_t, dq, w_qkv, embedded, grad_after, order, mask, gain, small, bias_up, *grads)
    return outs[0], outs[1:]


def swap(array, stage):
    if stage == 0:
        return lax.ppermute(array, "blk", [(0, 1), (1, 0)])
    if stage < 3:
        apart = lambda core: 2 if core == (stage == 2) else 4
        return lax.ppermute(array, ALL, [(i, i ^ apart(i % 2 == 1)) for i in range(OWNERS)])
    step = 4 << (stage - 3)
    return lax.ppermute(array, "dp", [(i, i ^ step) for i in range(OWNERS // 2)])


def crossed(parts):
    ahead, later = swap(parts[3], 0), swap(parts[2], 0)
    return [parts[0], later], [parts[1], ahead]


def cut(terms, at):
    halves = [jnp.split(x, 2, at) for x in terms]
    return [x[0] for x in halves], [x[1] for x in halves]


def join(groups):
    sums = [add(terms).astype(BF) for terms in groups]
    return jnp.concatenate([x.reshape(-1, x.shape[-1]) for x in sums], 0)


def part(received, groups):
    at = 0
    for terms in groups:
        shape = terms[0].shape
        size = math.prod(shape[:-1])
        terms.append(received[at : at + size].reshape(shape))
        at += size


def order_after(values, arrays):
    held = lax.optimization_barrier((tuple(values), tuple(arrays)))
    return held[0], held[1]


def natural(parts):
    columns = parts[0].shape[-1]
    array = jnp.stack([part.reshape(2, 4, -1, columns) for part in parts])
    array = array.reshape((2, 2, 2, 2, 2, -1, columns))
    return array.transpose((4, 3, 2, 1, 0, 5, 6)).reshape(-1, columns)


def body(
    paired,
    tubes, tube_mask, tube_order, cotangent, mask_token, pos_table, ln1_gain, ln1_bias, w_qkv, bias_q, bias_v,
    w_out, bias_out, ln2_gain, ln2_bias, w_up, bias_up, w_down, bias_down,
):
    clips, block, width = tubes.shape
    rows = clips * block
    blocks = lax.axis_size("blk")
    length = block * blocks
    owners = jnp.arange(OWNERS, dtype=jnp.int32)
    core = lax.axis_index("blk") if paired else 0
    me = lax.axis_index("dp") * 2 + core if paired else 0
    apart = jnp.bitwise_xor(owners, me)
    bit = lambda b: (apart >> b) & 1
    turned = jnp.bitwise_xor(core, bit(0)) if paired else 0
    first, second = jnp.where(turned == 0, bit(1), bit(2)), jnp.where(turned == 0, bit(2), bit(1))
    within = bit(0) * 4 + first * 2 + second
    layer = bit(3) * 2 + bit(4)
    table = jnp.concatenate([within * 4 + layer, within[:8], layer[::8]])

    order, mask = tube_order.reshape(1, rows), tube_mask.reshape(1, rows)
    cot = cotangent.reshape(rows, width)
    embedded, normed_t, queries, kv = embed(
        table, order, mask, pos_table, tubes.reshape(rows, width), (mask_token, ln1_gain, ln1_bias, bias_q, bias_v), w_qkv
    )
    held = [kv] + [
        lax.ppermute(kv, "blk", [(i, (i + s) % blocks) for i in range(blocks)]) for s in range(1, blocks)
    ]
    (attended, logs, result, grad_normed, bias_up_grad), near_parts, middle_parts, far_parts = forward(
        table, queries, held, embedded, (bias_out, ln2_gain, ln2_bias, bias_up), cot, w_out, w_up, w_down, clips
    )
    if paired:
        ahead, far_got, middle_got = swap(near_parts[3], 0), swap(far_parts[1], 0), swap(middle_parts[1], 0)
    output, grad_after, grad_att, dots, small, *out_parts = branch(
        table, attended, embedded, result, grad_normed, cot, w_out, bias_out, ln2_gain, bias_down
    )
    if paired:
        (grad_att,), (ahead, far_got, middle_got) = order_after((grad_att,), (ahead, far_got, middle_got))
        near = [near_parts[0], swap(near_parts[2], 0)]
        far, far_go = cut([far_parts[0], far_got], 1)
        middle, middle_go = cut([middle_parts[0], middle_got], 0)
        sent = [add(terms).astype(BF) for terms in ([near_parts[1], ahead], far_go, middle_go)]
        (grad_att,), (*sent, out_got) = order_after((grad_att,), (*sent, swap(out_parts[1], 0)))
        near.append(swap(sent[0], 1))
        far.append(swap(sent[1], 3))
        middle.append(swap(sent[2], 1))
        out = [x.reshape(2, 2, -1, width) for x in (out_parts[0], out_got)]
    home = lambda x, s: lax.ppermute(x, "blk", [((i + s) % blocks, i) for i in range(blocks)])
    dq, own, *away = attend_back(queries, grad_att, logs, dots, held, clips)
    if paired:
        away, (near[-1], far[-1]) = order_after(away, (near[-1], far[-1]))
        near, near_go = cut([x.reshape(NEAR_BLOCKS, 2, -1, width) for x in near], 1)
        out, out_go = cut(out, 1)
        near_got = swap(join([near_go, out_go]), 2)
        far, far_go = cut(far, 1)
        far_got = swap(join([far_go]), 4)
    grads = [home(x, s + 1) for s, x in enumerate(away)]
    grad_tubes, late_parts = last(
        table, normed_t, dq, w_qkv, embedded, grad_after, order, mask, ln1_gain, small, bias_up_grad,
        [own, *grads], length,
    )
    if paired:
        late_parts, (near_got, middle[-1]) = order_after(late_parts, (near_got, middle[-1]))
        late, late_go = crossed(late_parts)
        part(near_got, (near, out))
        part(far_got, (far,))
        near = [x.reshape(NEAR_BLOCKS, -1, width) for x in near]
        down, up = [x[:FF_STEPS].reshape(-1, width) for x in near], [x[FF_STEPS] for x in near]
        middle, middle_go = cut(middle, 0)
        middle_got = swap(add(middle_go).astype(BF), 2)
        late_sent = add(late_go).astype(BF)
        late.append(swap(late_sent, 1))
        far, far_go = cut(far, 1)
        out, out_go = cut(out, 0)
        far_got = swap(join([far_go, out_go]), 1)
        _, (far_got, middle_got) = order_after((late_sent,), (far_got, middle_got))
        part(far_got, (far, out))
        middle.append(middle_got)
        out = [x.reshape(-1, width) for x in out]
        for stage in (3, 4):
            sums = [cut(terms, 0) for terms in (down, up, middle, out)]
            down, up, middle, out = (keep for keep, _ in sums)
            part(swap(join([go for _, go in sums]), stage), (down, up, middle, out))
        far, far_go = cut(far, 1)
        part(swap(join([far_go]), 2), (far,))
        for stage in (2, 3, 4):
            late, go = cut(late, 0)
            late.append(swap(add(go).astype(BF), stage))
        grad_w_down, grad_w_out = add(down), add(out)
        grad_w_up = jnp.concatenate([add(up), add(middle), *add(far)], 1)
        late = add(late)
    else:
        spread = lambda array: lax.psum_scatter(array.astype(F32), ALL, scatter_dimension=0, tiled=True)
        quarters = lambda halves: [x for half in halves for x in jnp.split(half, 2, 0)]
        down = [x[:FF_STEPS].reshape(4, 2, -1, width).swapaxes(0, 1) for x in near_parts]
        far = [x.reshape(FAR_BLOCKS, 4, 2, 2, -1, width).transpose((2, 3, 1, 4, 0, 5)) for x in far_parts]
        far = [x.reshape(-1, FAR_BLOCKS * width) for half in far for x in half]
        up = [jnp.concatenate([x[FF_STEPS], y, z], 1) for x, y, z in zip(near_parts, quarters(middle_parts), far)]
        grad_w_down, grad_w_up = spread(natural(down)), spread(natural(up))
        grad_w_out, late = spread(natural(quarters(out_parts))), spread(natural(late_parts))
    grad_w_qkv, grad_pos, extra = jnp.split(late, [3 * width, 3 * width + length], 1)
    grad_bias_up = extra[:, 9:13].T.reshape(-1) if paired else spread(bias_up_grad[:FF_STEPS].reshape(-1))
    mask_grad, gain_one, shift_one, grad_bias_q, grad_bias_v, gain_two, shift_two, grad_bias_out, grad_bias_down = (
        extra[:, i] for i in range(9)
    )
    return (
        output.reshape(clips, block, width),
        grad_tubes.reshape(clips, block, width),
        mask_grad,
        grad_pos.T,
        gain_one,
        shift_one,
        grad_w_qkv,
        grad_bias_q,
        grad_bias_v,
        grad_w_out,
        grad_bias_out,
        gain_two,
        shift_two,
        grad_w_up,
        grad_bias_up,
        grad_w_down,
        grad_bias_down,
    )


def solution(mesh):
    split = P("dp", "blk", None)
    flat = P("dp", "blk")
    in_specs = (split, flat, flat, split) + (P(),) * 15
    one, two = P(ALL), P(ALL, None)
    out_specs = (split, split, one, P(None, ALL), one, one, two, one, one, two, one, one, one, two, one, two, one)
    paired = mesh.shape["blk"] == 2 and mesh.shape["dp"] == OWNERS // 2
    return jax.shard_map(
        functools.partial(body, paired), mesh=mesh, in_specs=in_specs, out_specs=out_specs, check_vma=False
    )
```

```python
import functools
import math

import jax
import jax.numpy as jnp
from jax import lax
from jax.experimental import pallas as pl
from jax.experimental.pallas import tpu as pltpu
from jax.sharding import PartitionSpec as P

HEADS = 12
HEAD_DIM = 64
PAIR = 2 * HEAD_DIM
EPSILON = 1e-06
SCORE_SCALE = 0.125
OWNERS = 32
EXTRA = 128
BF = jnp.bfloat16
F32 = jnp.float32
ALL = ("dp", "blk")
MIB = 1 << 20

NN = (((1,), (0,)), ((), ()))
NT = (((1,), (1,)), ((), ()))
TN = (((0,), (0,)), ((), ()))


def dot(left, right, dims=NN):
    return lax.dot_general(left, right, dims, preferred_element_type=F32)


def cost(micros):
    return pl.CostEstimate(flops=int(micros * 1e9), bytes_accessed=int(micros * 1e6), transcendentals=0)


def params(mib):
    return pltpu.CompilerParams(vmem_limit_bytes=mib * MIB)


def normalize(rows):
    centered = rows - jnp.mean(rows, -1, keepdims=True)
    inverse = lax.rsqrt(jnp.mean(centered * centered, -1, keepdims=True) + EPSILON)
    return centered * inverse, inverse


def norm_backward(grad, unit, inverse, gain):
    scaled = grad * gain
    return inverse * (
        scaled
        - jnp.mean(scaled, -1, keepdims=True)
        - unit * jnp.mean(scaled * unit, -1, keepdims=True)
    )


def lane_columns(row):
    return jnp.transpose(jnp.broadcast_to(row, (128, row.shape[1])), (1, 0))


def store_quarters(refs, array):
    quarter = array.shape[0] // 4
    for i, ref in enumerate(refs):
        ref[...] = array[i * quarter : (i + 1) * quarter].astype(BF)


SLOT, WITHIN, LAYER = 0, OWNERS, OWNERS + 8


def place_blocks(table_ref, transposed, slots):
    size = transposed.shape[0] // OWNERS
    for owner in range(OWNERS):
        slots[table_ref[SLOT + owner]] = transposed[owner * size : (owner + 1) * size]


def flat(ref):
    return ref[...].reshape(1, -1)


def add(terms):
    return functools.reduce(jnp.add, [x.astype(F32) for x in terms])


def total(rows):
    return jnp.sum(rows, 0, keepdims=True)


VMEM = pl.BlockSpec(memory_space=pltpu.VMEM)
SMEM = pl.BlockSpec(memory_space=pltpu.SMEM)
ANY = pl.BlockSpec(memory_space=pl.ANY)
HBM = pl.BlockSpec(memory_space=pltpu.HBM)


def in_hbm(array):
    return pltpu.with_memory_space_constraint(array, pltpu.HBM)


def one_hot(order_ref, length):
    order = lane_columns(order_ref[...].astype(F32))
    lanes = lax.broadcasted_iota(jnp.int32, order.shape, 1).astype(F32)
    return jnp.concatenate([jnp.where(order == lanes + at, 1.0, 0.0).astype(BF) for at in range(0, length, 128)], 1)


def wide_mask(mask_ref, width):
    mask = lane_columns(mask_ref[...].astype(F32))
    return jnp.concatenate([mask] * (width // 128), 1) > 0.5


def embed_kernel(table_ref, *refs):
    sources, refs = refs[:10], refs[10:]
    (emb_ref, normed_t_ref, q_ref, kv_ref), refs = refs[:4], refs[4:]
    places, (normed, slots, w, sems) = refs[:9], refs[9:]
    order_ref, mask_ref, positions_ref, tubes_ref, token_ref, gain_ref, shift_ref, bias_q_ref, bias_v_ref = places
    rows, width = tubes_ref.shape
    loads = [pltpu.make_async_copy(source, place, sems.at[i]) for i, (source, place) in enumerate(zip(sources, places))]
    w_ref = sources[9]
    loads += [
        pltpu.make_async_copy(w_ref.at[:, pl.ds(part * width, width)], w.at[part], sems.at[9 + part]) for part in range(3)
    ]
    for load in loads:
        load.start()
    loads[0].wait()
    hot = one_hot(order_ref, positions_ref.shape[0])
    for load in loads[1:9]:
        load.wait()
    masks = wide_mask(mask_ref, width)
    embedded = jnp.where(masks, flat(token_ref), tubes_ref[...].astype(F32)) + dot(hot, positions_ref[...])
    emb_ref[...] = embedded
    unit, _ = normalize(embedded)
    normed_rows = unit * flat(gain_ref) + flat(shift_ref)
    normed[...] = normed_rows.astype(BF)
    for load in loads[9:]:
        load.wait()
    kv_ref[:, :width] = dot(normed[...], w[1]).astype(BF)
    kv_ref[:, width:] = (dot(normed[...], w[2]) + flat(bias_v_ref)).astype(BF)
    queries = (dot(normed[...], w[0]) + flat(bias_q_ref)).astype(BF)
    q_ref[...] = (queries.astype(F32) * SCORE_SCALE).astype(BF)
    place_blocks(table_ref, jnp.transpose(normed_rows, (1, 0)), slots)
    normed_t_ref[...] = slots[...].reshape(width, rows).astype(BF)


def embed(table, order, mask, positions, tubes, vectors, w_qkv):
    rows, width = tubes.shape
    sources = (order, mask, positions, tubes, *vectors)
    return pl.pallas_call(
        embed_kernel,
        in_specs=[SMEM] + [HBM] * 10,
        out_specs=[VMEM] * 4,
        out_shape=[
            jax.ShapeDtypeStruct((rows, width), F32),
            jax.ShapeDtypeStruct((width, rows), BF),
            jax.ShapeDtypeStruct((rows, width), BF),
            jax.ShapeDtypeStruct((rows, 2 * width), BF),
        ],
        scratch_shapes=[pltpu.VMEM(x.shape, x.dtype) for x in sources]
        + [
            pltpu.VMEM((rows, width), BF),
            pltpu.VMEM((OWNERS, width // OWNERS, rows), F32),
            pltpu.VMEM((3, width, width), BF),
            pltpu.SemaphoreType.DMA((12,)),
        ],
        compiler_params=params(24),
        cost_estimate=cost(6),
        name="embed",
    )(table, *[in_hbm(x) for x in (*sources, w_qkv)])


def attend_pair(queries_ref, keys, values, tile, out_ref, log_ref):
    low_half = lax.broadcasted_iota(jnp.int32, (1, PAIR), 1) < HEAD_DIM
    one, zero = jnp.ones((), BF), jnp.zeros((), BF)
    value_halves = [jnp.where(low_half, values, one), jnp.where(low_half, one, values)]
    items = [(at, half) for at in range(0, queries_ref.shape[0], tile) for half in range(2)]

    def score(at, half):
        queries = queries_ref[at : at + tile, :]
        own = jnp.where(low_half, queries, zero) if half == 0 else jnp.where(low_half, zero, queries)
        return dot(own, keys, NT)

    ahead = score(*items[0])
    for i, (at, half) in enumerate(items):
        scores = ahead
        if i + 1 < len(items):
            ahead = score(*items[i + 1])
        if half == 0:
            tops, mixed = [], []
        top = jnp.max(scores, -1, keepdims=True)
        weights = jnp.exp(scores - top).astype(BF)
        tops.append(top)
        mixed.append(dot(weights, value_halves[half]))
        if half == 0:
            continue
        sums = pltpu.roll(jnp.where(low_half, mixed[1], mixed[0]), HEAD_DIM, 1)
        out_ref[at : at + tile, :] = jnp.where(low_half, mixed[0], mixed[1]) / sums
        logs = jnp.where(low_half, tops[0], tops[1]) + jnp.log(sums)
        logs = jnp.transpose(logs, (1, 0))
        log_ref[0:1, at : at + tile] = logs[0:1]
        log_ref[1:2, at : at + tile] = logs[HEAD_DIM : HEAD_DIM + 1]


def gelu_terms(x):
    bell = jnp.exp(x * x * -0.5)
    t = 1.0 / (1.0 + jnp.abs(x) * (0.3275911 * math.sqrt(0.5)))
    a1, a2, a3, a4, a5 = (0.5 * a for a in (0.254829592, -0.284496736, 1.421413741, -1.453152027, 1.061405429))
    tail = t * (a1 + t * (a2 + t * (a3 + t * (a4 + t * a5)))) * bell
    cdf = jnp.where(x >= 0.0, 1.0 - tail, tail)
    return x * cdf, cdf + x * bell * (1.0 / math.sqrt(2.0 * math.pi))


FF_STEPS = 4
NEAR_BLOCKS, FAR_BLOCKS = FF_STEPS + 1, FF_STEPS - 2


def pair_loop(clips, pairs, block, work):
    def step(i, carry):
        clip, pair = lax.div(i, pairs), lax.rem(i, pairs)
        at = pl.ds(pl.multiple_of(clip * block, block), block)
        work(clip, pair, at, lambda off: pl.ds(pl.multiple_of((pair + off) * PAIR, PAIR), PAIR))
        return carry

    lax.fori_loop(0, clips * pairs, step, 0, unroll=2)


def after_attention(att_ref, emb_ref, w_ref, bias_ref):
    return emb_ref[...] + dot(att_ref[...].astype(BF), w_ref[...]) + flat(bias_ref)


def forward_kernel(clips, blocks, tile, table_ref, q_ref, *refs):
    held_refs = refs[:blocks]
    (
        emb_ref, bias_out_ref, gain_ref, shift_ref, bias_in_ref, cot_ref, w_out_ref, w_up_ref, w_down_ref,
        att, log_ref, result, grad_normed, bias_up_ref,
    ) = refs[blocks : 14 + blocks]
    near_refs, middle_refs, far_refs = (refs[14 + blocks :][i:j] for i, j in ((0, 4), (4, 6), (6, 8)))
    normed, normed_t, slots, act_slots, act_all, pre_all, w_up, w_down, stage, in_sems, out_sems = refs[22 + blocks :]
    rows, width = emb_ref.shape
    pairs = width // PAIR
    quarter = width // 4
    loads = []
    for f in range(FF_STEPS):
        at = pl.ds(f * width, width)
        loads.append(
            [
                pltpu.make_async_copy(w_up_ref.at[:, at], w_up.at[f], in_sems.at[f, 0]),
                pltpu.make_async_copy(w_down_ref.at[at, :], w_down.at[f], in_sems.at[f, 1]),
            ]
        )
        for load in loads[f]:
            load.start()

    def attend_one(clip, pair, at, lanes):
        keys = jnp.concatenate([ref[at, lanes(0)] for ref in held_refs], 0)
        values = jnp.concatenate([ref[at, lanes(pairs)] for ref in held_refs], 0)
        attend_pair(q_ref.at[at, lanes(0)], keys, values, tile, att.at[at, lanes(0)], log_ref.at[clip, pair])

    pair_loop(clips, pairs, rows // clips, attend_one)

    after = after_attention(att, emb_ref, w_out_ref, bias_out_ref)
    unit_rows, inverse_rows = normalize(after)
    normed_rows = unit_rows * flat(gain_ref) + flat(shift_ref)
    normed[...] = normed_rows.astype(BF)
    result[...] = after
    place_blocks(table_ref, jnp.transpose(normed_rows, (1, 0)), slots)
    normed_t[...] = slots[...].reshape(width, rows).astype(BF)

    stores = {}

    def store(f, kind, array):
        for old in stores.pop((kind, f % 2), ()):
            old.wait()
        copies = []
        parts = [array[i * quarter : (i + 1) * quarter] for i in range(4)]
        if kind == 0:
            targets = [ref.at[table_ref[LAYER + f]] for ref in near_refs]
        elif f == 0:
            targets = [ref.at[FF_STEPS] for ref in near_refs]
        elif f == 1:
            targets = [middle_refs[i // 2].at[pl.ds(i % 2 * quarter, quarter)] for i in range(4)]
        else:
            targets = [far_refs[i // 2].at[f - 2, pl.ds(i % 2 * quarter, quarter)] for i in range(4)]
            owner = width // OWNERS
            by_z = [i * 16 + xy * 4 + z for i in range(2) for z in range(4) for xy in range(4)]
            parts = [
                jnp.concatenate([array[slot * owner : (slot + 1) * owner] for slot in by_z[i * 8 : i * 8 + 8]], 0)
                for i in range(4)
            ]
        for i, (part, target) in enumerate(zip(parts, targets)):
            place = stage.at[kind, f % 2, i]
            place[...] = part.astype(BF)
            copies.append(pltpu.make_async_copy(place, target, out_sems.at[kind, f % 2, i]))
            copies[-1].start()
        stores[kind, f % 2] = copies

    halves = 2
    span = rows // halves
    own = OWNERS // FF_STEPS

    def products(f, h):
        rows_at = slice(h * span, (h + 1) * span)
        bias = flat(bias_in_ref)[:, f * width : (f + 1) * width]
        return dot(normed[rows_at, :], w_up[f]) + bias, dot(cot_ref[rows_at, :], w_down[f], NT)

    def activate(f, h, pre_act, grad_active):
        active, slope = gelu_terms(pre_act)
        grad_pre = (grad_active * slope).astype(BF)
        rows_at = slice(h * span, (h + 1) * span)
        act_all[f % 2, rows_at, :] = active.astype(BF)
        pre_all[f % 2, rows_at, :] = grad_pre
        active_t = jnp.transpose(active, (1, 0)).astype(BF)
        for k in range(own):
            act_slots[f % 2, table_ref[WITHIN + k], :, rows_at] = active_t[k * (width // own) : (k + 1) * (width // own)]

    def tasks(f):
        held = {}

        def add_up(h):
            rows_at = slice(h * span, (h + 1) * span)
            result[rows_at, :] += dot(act_all[f % 2, rows_at, :], w_down[f])
            term = dot(pre_all[f % 2, rows_at, :], w_up[f], NT)
            if f == 0:
                grad_normed[rows_at, :] = term
            else:
                grad_normed[rows_at, :] += term

        def grad_part(kind, p):
            at = slice(p * width // 3, (p + 1) * width // 3)
            left = normed_t[at, :] if kind else act_slots[f % 2].reshape(width, rows)[at, :]
            right = pre_all[f % 2] if kind else cot_ref[...]
            held[kind, p] = dot(left, right)
            if p == 2:
                store(f, kind, jnp.concatenate([held[kind, i] for i in range(3)], 0))

        def bias_sum():
            bias_up_ref[f : f + 1, :] = total(pre_all[f % 2].astype(F32))

        out = [functools.partial(add_up, h) for h in range(halves)]
        out += [functools.partial(grad_part, kind, p) for kind in (1, 0) for p in range(3)]
        return out + [bias_sum]

    waiting = []
    for f in range(FF_STEPS):
        for load in loads[f]:
            load.wait()
        each = -(-len(waiting) // halves)
        ahead = products(f, 0)
        for h in range(halves):
            now = ahead
            if h + 1 < halves:
                ahead = products(f, h + 1)
            batch, waiting = waiting[:each], waiting[each:]
            for task in batch[: len(batch) // 2]:
                task()
            activate(f, h, *now)
            for task in batch[len(batch) // 2 :]:
                task()
        waiting = tasks(f)
    for task in waiting:
        task()
    bias_up_ref[FF_STEPS:, :] = jnp.zeros((8 - FF_STEPS, width), F32)
    for copies in stores.values():
        for copy in copies:
            copy.wait()


def forward(table, queries, held, embedded, vectors, cot, w_out, w_up, w_down, clips):
    rows, width = queries.shape
    block = rows // clips
    pairs = width // PAIR
    blocks = len(held)
    quarter = width // 4
    big = pltpu.VMEM((rows, width), F32)
    outs = pl.pallas_call(
        functools.partial(forward_kernel, clips, blocks, min(block, 256)),
        in_specs=[SMEM] + [VMEM] * (1 + blocks + 7) + [HBM] * 2,
        out_specs=[VMEM] * 5 + [HBM] * 8,
        out_shape=[
            big,
            jax.ShapeDtypeStruct((clips, pairs, 2, block), F32),
            big,
            big,
            jax.ShapeDtypeStruct((8, width), F32),
        ]
        + [pltpu.HBM((NEAR_BLOCKS, quarter, width), BF)] * 4
        + [pltpu.HBM((2 * quarter, width), BF)] * 2
        + [pltpu.HBM((FAR_BLOCKS, 2 * quarter, width), BF)] * 2,
        scratch_shapes=[
            pltpu.VMEM((rows, width), BF), pltpu.VMEM((width, rows), BF),
            pltpu.VMEM((OWNERS, width // OWNERS, rows), F32), pltpu.VMEM((2, 8, width // 8, rows), BF),
            pltpu.VMEM((2, rows, width), BF), pltpu.VMEM((2, rows, width), BF),
            pltpu.VMEM((FF_STEPS, width, width), BF), pltpu.VMEM((FF_STEPS, width, width), BF),
            pltpu.VMEM((2, 2, 4, quarter, width), BF),
            pltpu.SemaphoreType.DMA((FF_STEPS, 2)), pltpu.SemaphoreType.DMA((2, 2, 4)),
        ],
        compiler_params=params(32),
        cost_estimate=cost(40),
        name="forward",
    )(table, queries, *held, embedded, *vectors, cot, w_out, in_hbm(w_up), in_hbm(w_down))
    return outs[:5], outs[5:9], outs[9:11], outs[11:]


def branch_kernel(
    table_ref, att_ref, emb_ref, result_ref, grad_normed_ref, cot_ref, w_out_ref, bias_out_ref, gain_ref, bias_down_ref,
    output_ref, grad_after_ref, grad_att_ref, dots_ref, small_ref, here_ref, there_ref, slots,
):
    rows, width = emb_ref.shape
    place_blocks(table_ref, jnp.transpose(att_ref[...], (1, 0)), slots)
    output_ref[...] = (result_ref[...] + flat(bias_down_ref)).astype(BF)
    cot = cot_ref[...].astype(F32)
    grad_rows = grad_normed_ref[...]
    unit_rows, inverse_rows = normalize(after_attention(att_ref, emb_ref, w_out_ref, bias_out_ref))
    grad_after = cot + norm_backward(grad_rows, unit_rows, inverse_rows, flat(gain_ref))
    grad_after_ref[...] = grad_after
    branch = grad_after.astype(BF)
    grad_att = dot(branch, w_out_ref[...], NT).astype(BF)
    grad_att_ref[...] = grad_att
    grad_out = dot(slots[...].reshape(width, rows).astype(BF), branch).astype(BF)
    here_ref[...] = grad_out[: width // 2]
    there_ref[...] = grad_out[width // 2 :]
    small_ref[...] = jnp.concatenate(
        [
            total(grad_rows * unit_rows), total(grad_rows), total(branch.astype(F32)), total(cot),
            jnp.zeros((4, width), F32),
        ],
        0,
    )
    product = jnp.transpose(grad_att.astype(F32) * att_ref[...], (1, 0))
    for head in range(width // HEAD_DIM):
        dots_ref[head // 2, head % 2 : head % 2 + 1, :] = total(product[head * HEAD_DIM : (head + 1) * HEAD_DIM])


def branch(table, attended, embedded, result, grad_normed, cot, w_out, bias_out, gain, bias_down):
    rows, width = embedded.shape
    outs = pl.pallas_call(
        branch_kernel,
        in_specs=[SMEM] + [VMEM] * 9,
        out_specs=[VMEM] * 7,
        out_shape=[
            jax.ShapeDtypeStruct((rows, width), BF),
            jax.ShapeDtypeStruct((rows, width), F32),
            jax.ShapeDtypeStruct((rows, width), BF),
            jax.ShapeDtypeStruct((width // PAIR, 2, rows), F32),
            jax.ShapeDtypeStruct((8, width), F32),
            *[jax.ShapeDtypeStruct((width // 2, width), BF)] * 2,
        ],
        scratch_shapes=[pltpu.VMEM((OWNERS, width // OWNERS, rows), F32)],
        compiler_params=params(24),
        cost_estimate=cost(5),
        name="branch",
    )(table, attended, embedded, result, grad_normed, cot, w_out, bias_out, gain, bias_down)
    return outs


def attend_back_kernel(clips, tile, q_ref, grad_ref, log_ref, dots_ref, *refs):
    blocks = (len(refs) - 1) // 2
    held_refs, dq_ref, out_refs = refs[:blocks], refs[blocks], refs[blocks + 1 :]
    rows, width = q_ref.shape
    pairs = width // PAIR
    size = rows // clips
    low_half = lax.broadcasted_iota(jnp.int32, (1, PAIR), 1) < HEAD_DIM
    zero = jnp.zeros((), BF)
    pick = lambda x, half: jnp.where(low_half, x, zero) if half == 0 else jnp.where(low_half, zero, x)
    items = [(block, at, half) for block in range(blocks) for at in range(0, size, tile) for half in range(2)]

    def one(clip, pair, rows_at, lanes):
        queries, grads = q_ref[rows_at, lanes(0)], grad_ref[rows_at, lanes(0)]
        dots = [dots_ref[pair, half : half + 1, rows_at] for half in range(2)]
        logs = [log_ref[clip, pair, half : half + 1, :] for half in range(2)]

        def products(block, at, half):
            ref = held_refs[block].at[rows_at, :]
            keys = pick(ref[at : at + tile, lanes(0)], half)
            values = pick(ref[at : at + tile, lanes(pairs)], half)
            return keys, dot(keys, queries, NT), dot(values, grads, NT)

        ahead = products(*items[0])
        dq_t = jnp.zeros((PAIR, size), F32)
        for i, (block, at, half) in enumerate(items):
            own_keys, scores, grad_probs = ahead
            if i + 1 < len(items):
                ahead = products(*items[i + 1])
            probs = jnp.exp(scores - logs[half])
            grad_scores = (probs * (grad_probs - dots[half])).astype(BF)
            if half == 0:
                dkeys, dvalues = [], []
            dvalues.append(dot(probs.astype(BF), grads))
            dkeys.append(dot(grad_scores, queries))
            dq_t += dot(own_keys, grad_scores, TN)
            if half == 1:
                for j, pair_of in enumerate((dkeys, dvalues)):
                    ref = out_refs[block].at[j, rows_at, :]
                    ref[at : at + tile, lanes(0)] = jnp.where(low_half, *pair_of).astype(ref.dtype)
        dq_ref[rows_at, lanes(0)] = (jnp.transpose(dq_t, (1, 0)) * SCORE_SCALE).astype(BF)

    pair_loop(clips, pairs, size, one)


def attend_back(queries, grads, logs, dots, held, clips):
    rows, width = queries.shape
    blocks = len(held)
    return pl.pallas_call(
        functools.partial(attend_back_kernel, clips, min(rows // clips, 512)),
        in_specs=[VMEM] * (4 + blocks),
        out_specs=[VMEM] * (1 + blocks),
        out_shape=[jax.ShapeDtypeStruct((rows, width), BF), jax.ShapeDtypeStruct((2, rows, width), F32)]
        + [jax.ShapeDtypeStruct((2, rows, width), BF)] * (blocks - 1),
        compiler_params=params(16),
        cost_estimate=cost(17),
        name="attend_back",
    )(queries, grads, logs, dots, *held)


def last_kernel(
    parts, table_ref, normed_t_ref, dq_ref, w_ref, emb_ref, grad_after_ref, order_ref, mask_ref, gain_ref, small_ref,
    bias_up_ref, *refs,
):
    grad_refs, tubes_ref, out_refs, (slots, extra_slots) = refs[:parts], refs[parts], refs[parts + 1 : parts + 5], refs[parts + 5 :]
    rows, width = emb_ref.shape
    store = lambda at, array: store_quarters([ref.at[:, at : at + array.shape[1]] for ref in out_refs], array)
    sums, grad_rows = [], 0.0
    for part in range(3):
        if part == 0:
            packed = dq_ref[...]
        else:
            packed = add([ref[part - 1] for ref in grad_refs]).astype(BF)
        sums.append(total(packed.astype(F32)))
        store(part * width, dot(normed_t_ref[...], packed))
        grad_rows += dot(packed, w_ref[:, part * width : (part + 1) * width], NT)
    grad_after = grad_after_ref[...]
    unit, inverse = normalize(emb_ref[...])
    grad = grad_after + norm_backward(grad_rows, unit, inverse, flat(gain_ref))
    kept = jnp.where(wide_mask(mask_ref, width), 0.0, grad)
    tubes_ref[...] = kept
    place_blocks(table_ref, jnp.transpose(grad, (1, 0)), slots)
    length = out_refs[0].shape[1] - 3 * width - EXTRA
    store(3 * width, dot(slots[...].reshape(width, rows).astype(BF), one_hot(order_ref, length)))
    stacked = jnp.concatenate(
        [
            total(grad - kept), total(grad_rows * unit), total(grad_rows), sums[0], sums[2],
            small_ref[0:4, :], bias_up_ref[0:FF_STEPS, :], jnp.zeros((EXTRA - 9 - FF_STEPS, width), F32),
        ],
        0,
    )
    extra = jnp.transpose(stacked, (1, 0))
    lanes = lax.broadcasted_iota(jnp.int32, (1, EXTRA), 1)
    size = width // OWNERS
    for feed in range(FF_STEPS):
        column = jnp.broadcast_to(extra[:, 9 + feed : 10 + feed], extra.shape)
        for i in range(OWNERS // FF_STEPS):
            owner = feed * (OWNERS // FF_STEPS) + i
            tile = extra[owner * size : (owner + 1) * size]
            for k in range(4):
                tile = jnp.where(lanes == 9 + k, column[(i * 4 + k) * size : (i * 4 + k + 1) * size], tile)
            extra_slots[table_ref[SLOT + owner]] = tile
    store(3 * width + length, extra_slots[...].reshape(width, EXTRA))


def last(table, normed_t, dq, w_qkv, embedded, grad_after, order, mask, gain, small, bias_up, grads, length):
    rows, width = embedded.shape
    outs = pl.pallas_call(
        functools.partial(last_kernel, len(grads)),
        in_specs=[SMEM] + [VMEM] * (10 + len(grads)),
        out_specs=[VMEM] * 5,
        out_shape=[jax.ShapeDtypeStruct((rows, width), F32)]
        + [jax.ShapeDtypeStruct((width // 4, 3 * width + length + EXTRA), BF)] * 4,
        scratch_shapes=[
            pltpu.VMEM((OWNERS, width // OWNERS, rows), F32),
            pltpu.VMEM((OWNERS, width // OWNERS, EXTRA), F32),
        ],
        compiler_params=params(24),
        cost_estimate=cost(8),
        name="last",
    )(table, normed_t, dq, w_qkv, embedded, grad_after, order, mask, gain, small, bias_up, *grads)
    return outs[0], outs[1:]


def swap(array, stage):
    if stage == 0:
        return lax.ppermute(array, "blk", [(0, 1), (1, 0)])
    if stage < 3:
        apart = lambda core: 2 if core == (stage == 2) else 4
        return lax.ppermute(array, ALL, [(i, i ^ apart(i % 2 == 1)) for i in range(OWNERS)])
    step = 4 << (stage - 3)
    return lax.ppermute(array, "dp", [(i, i ^ step) for i in range(OWNERS // 2)])


def crossed(parts):
    ahead, later = swap(parts[3], 0), swap(parts[2], 0)
    return [parts[0], later], [parts[1], ahead]


def cut(terms, at):
    halves = [jnp.split(x, 2, at) for x in terms]
    return [x[0] for x in halves], [x[1] for x in halves]


def join(groups):
    sums = [add(terms).astype(BF) for terms in groups]
    return jnp.concatenate([x.reshape(-1, x.shape[-1]) for x in sums], 0)


def part(received, groups):
    at = 0
    for terms in groups:
        shape = terms[0].shape
        size = math.prod(shape[:-1])
        terms.append(received[at : at + size].reshape(shape))
        at += size


def order_after(values, arrays):
    held = lax.optimization_barrier((tuple(values), tuple(arrays)))
    return held[0], held[1]


def natural(parts):
    columns = parts[0].shape[-1]
    array = jnp.stack([part.reshape(2, 4, -1, columns) for part in parts])
    array = array.reshape((2, 2, 2, 2, 2, -1, columns))
    return array.transpose((4, 3, 2, 1, 0, 5, 6)).reshape(-1, columns)


def body(
    paired,
    tubes, tube_mask, tube_order, cotangent, mask_token, pos_table, ln1_gain, ln1_bias, w_qkv, bias_q, bias_v,
    w_out, bias_out, ln2_gain, ln2_bias, w_up, bias_up, w_down, bias_down,
):
    clips, block, width = tubes.shape
    rows = clips * block
    blocks = lax.axis_size("blk")
    length = block * blocks
    owners = jnp.arange(OWNERS, dtype=jnp.int32)
    core = lax.axis_index("blk") if paired else 0
    me = lax.axis_index("dp") * 2 + core if paired else 0
    apart = jnp.bitwise_xor(owners, me)
    bit = lambda b: (apart >> b) & 1
    turned = jnp.bitwise_xor(core, bit(0)) if paired else 0
    first, second = jnp.where(turned == 0, bit(1), bit(2)), jnp.where(turned == 0, bit(2), bit(1))
    within = bit(0) * 4 + first * 2 + second
    layer = bit(3) * 2 + bit(4)
    table = jnp.concatenate([within * 4 + layer, within[:8], layer[::8]])

    order, mask = tube_order.reshape(1, rows), tube_mask.reshape(1, rows)
    cot = cotangent.reshape(rows, width)
    embedded, normed_t, queries, kv = embed(
        table, order, mask, pos_table, tubes.reshape(rows, width), (mask_token, ln1_gain, ln1_bias, bias_q, bias_v), w_qkv
    )
    held = [kv] + [
        lax.ppermute(kv, "blk", [(i, (i + s) % blocks) for i in range(blocks)]) for s in range(1, blocks)
    ]
    (attended, logs, result, grad_normed, bias_up_grad), near_parts, middle_parts, far_parts = forward(
        table, queries, held, embedded, (bias_out, ln2_gain, ln2_bias, bias_up), cot, w_out, w_up, w_down, clips
    )
    if paired:
        ahead, far_got, middle_got = swap(near_parts[3], 0), swap(far_parts[1], 0), swap(middle_parts[1], 0)
    output, grad_after, grad_att, dots, small, *out_parts = branch(
        table, attended, embedded, result, grad_normed, cot, w_out, bias_out, ln2_gain, bias_down
    )
    if paired:
        (grad_att,), (ahead, far_got) = order_after((grad_att,), (ahead, far_got))
        near = [near_parts[0], swap(near_parts[2], 0)]
        far, far_go = cut([far_parts[0], far_got], 1)
        sent = [add(terms).astype(BF) for terms in ([near_parts[1], ahead], far_go)]
        (grad_att,), (*sent, out_got, middle_got) = order_after((grad_att,), (*sent, swap(out_parts[1], 0), middle_got))
        near.append(swap(sent[0], 1))
        far.append(swap(sent[1], 3))
        middle = [middle_parts[0], middle_got]
        out = [x.reshape(2, 2, -1, width) for x in (out_parts[0], out_got)]
    home = lambda x, s: lax.ppermute(x, "blk", [((i + s) % blocks, i) for i in range(blocks)])
    dq, own, *away = attend_back(queries, grad_att, logs, dots, held, clips)
    if paired:
        away, (near[-1], far[-1]) = order_after(away, (near[-1], far[-1]))
        near, near_go = cut([x.reshape(NEAR_BLOCKS, 2, -1, width) for x in near], 1)
        out, out_go = cut(out, 1)
        near_got = swap(join([near_go, out_go]), 2)
        far, far_go = cut(far, 1)
        far_got = swap(join([far_go]), 4)
    grads = [home(x, s + 1) for s, x in enumerate(away)]
    grad_tubes, late_parts = last(
        table, normed_t, dq, w_qkv, embedded, grad_after, order, mask, ln1_gain, small, bias_up_grad,
        [own, *grads], length,
    )
    if paired:
        late_parts, (near_got,) = order_after(late_parts, (near_got,))
        late, late_go = crossed(late_parts)
        part(near_got, (near, out))
        near = [x.reshape(NEAR_BLOCKS, -1, width) for x in near]
        out = [x.reshape(2, -1, width) for x in out]
        down, up = [x[:FF_STEPS].reshape(-1, width) for x in near], [x[FF_STEPS] for x in near]
        late_sent = add(late_go).astype(BF)
        late.append(swap(late_sent, 1))
        sums = [cut(terms, 0) for terms in (down, up)]
        down, up = (keep for keep, _ in sums)
        down_got = swap(join([go for _, go in sums]), 3)
        part(far_got, (far,))
        far, far_go = cut(far, 1)
        middle, middle_go = cut(middle, 0)
        out, out_go = cut(out, 0)
        far_got = swap(join([far_go, middle_go, out_go]), 1)
        _, (far_got, down_got) = order_after((late_sent,), (far_got, down_got))
        part(down_got, (down, up))
        sums = [cut(terms, 0) for terms in (down, up)]
        down, up = (keep for keep, _ in sums)
        part(swap(join([go for _, go in sums]), 4), (down, up))
        part(far_got, (far, middle, out))
        out = [x.reshape(-1, width) for x in out]
        far, far_go = cut(far, 1)
        middle, middle_go = cut(middle, 0)
        part(swap(join([far_go, middle_go]), 2), (far, middle))
        for stage in (3, 4):
            sums = [cut(terms, 0) for terms in (middle, out)]
            middle, out = (keep for keep, _ in sums)
            part(swap(join([go for _, go in sums]), stage), (middle, out))
        for stage in (2, 3, 4):
            late, go = cut(late, 0)
            late.append(swap(add(go).astype(BF), stage))
        grad_w_down, grad_w_out = add(down), add(out)
        grad_w_up = jnp.concatenate([add(up), add(middle), *add(far)], 1)
        late = add(late)
    else:
        spread = lambda array: lax.psum_scatter(array.astype(F32), ALL, scatter_dimension=0, tiled=True)
        quarters = lambda halves: [x for half in halves for x in jnp.split(half, 2, 0)]
        down = [x[:FF_STEPS].reshape(4, 2, -1, width).swapaxes(0, 1) for x in near_parts]
        far = [x.reshape(FAR_BLOCKS, 4, 2, 2, -1, width).transpose((2, 3, 1, 4, 0, 5)) for x in far_parts]
        far = [x.reshape(-1, FAR_BLOCKS * width) for half in far for x in half]
        up = [jnp.concatenate([x[FF_STEPS], y, z], 1) for x, y, z in zip(near_parts, quarters(middle_parts), far)]
        grad_w_down, grad_w_up = spread(natural(down)), spread(natural(up))
        grad_w_out, late = spread(natural(quarters(out_parts))), spread(natural(late_parts))
    grad_w_qkv, grad_pos, extra = jnp.split(late, [3 * width, 3 * width + length], 1)
    grad_bias_up = extra[:, 9:13].T.reshape(-1) if paired else spread(bias_up_grad[:FF_STEPS].reshape(-1))
    mask_grad, gain_one, shift_one, grad_bias_q, grad_bias_v, gain_two, shift_two, grad_bias_out, grad_bias_down = (
        extra[:, i] for i in range(9)
    )
    return (
        output.reshape(clips, block, width),
        grad_tubes.reshape(clips, block, width),
        mask_grad,
        grad_pos.T,
        gain_one,
        shift_one,
        grad_w_qkv,
        grad_bias_q,
        grad_bias_v,
        grad_w_out,
        grad_bias_out,
        gain_two,
        shift_two,
        grad_w_up,
        grad_bias_up,
        grad_w_down,
        grad_bias_down,
    )


def solution(mesh):
    split = P("dp", "blk", None)
    flat = P("dp", "blk")
    in_specs = (split, flat, flat, split) + (P(),) * 15
    one, two = P(ALL), P(ALL, None)
    out_specs = (split, split, one, P(None, ALL), one, one, two, one, one, two, one, one, one, two, one, two, one)
    paired = mesh.shape["blk"] == 2 and mesh.shape["dp"] == OWNERS // 2
    return jax.shard_map(
        functools.partial(body, paired), mesh=mesh, in_specs=in_specs, out_specs=out_specs, check_vma=False
    )
```
